32 devices in a mesh: event: 4 (over x, core), space: 8 (over z, y).
Axes of the slice: x: 2, y: 2, z: 4, core: 2. Of those that a mesh axis runs over, the one named last changes fastest.
Arguments:
- state_now: float32 [4, 64, 16, 512], P('event', 'space'), may hold values from -6 to 6
- state_prev: float32 [4, 64, 16, 512], P('event', 'space'), may hold values from -6 to 6
- adjoint_now: float32 [4, 64, 16, 512], P('event', 'space'), may hold values from -1.8 to 1.8
- adjoint_next: float32 [4, 64, 16, 512], P('event', 'space'), may hold values from -1.8 to 1.8
- modulus: float32 [5, 16, 5, 4, 5, 128], P(None, 'space'), may hold values from 0.5 to 2
- density: float32 [64, 16, 512], P('space'), may hold values from 0.5 to 2
- receivers: int32 [1024], P('space'), may hold values from 0 to 65535
- observed: float32 [4, 3, 1024], P('event', None, 'space'), may hold values from -12 to 12
Outputs:
- kernel: float32 [5, 16, 5, 4, 5, 128], P(None, 'space', None, 'event')
- misfit: float32 [4], P('event')
The draws below stay inside these ranges and needn't reach their ends.
Inputs may be any that keep to these rules, and one draw needn't show every extreme that they name: A node of the receiver's own slab, numbered with the third index fastest over 8 x 16 x 512 nodes; two receivers may share a node.
All inputs are finite; a program needn't handle non-finite values. Where the reference program divides by a largest or mean magnitude, that divisor is 1e-20 or more.
Results may differ from the reference program's by a relative error of at most 0.00011.
Values sent between devices are 32-bit elements; how exact they have to be, the bound alone decides.
A program may use at most 64 MiB of HBM per device.

```python
import math
import jax
import jax.numpy as jnp
import numpy as np
from jax import lax

NODES_1D = 5
EXD = 2
EY = 4
EZ = 128
REC_DEV = 128
NT = 3
EX = 16
EVENTS = 4
RECEIVERS = 1024
NX = 64
NY = 16
NZ = 512
NODES_DEV = 65536


def draw_observed(key, part):
    position = jnp.arange(RECEIVERS, dtype=jnp.float32)
    rising = 1.0 + 2.0 * position / (RECEIVERS - 1)
    values = jax.random.truncated_normal(key, -4.0, 4.0, (EVENTS, NT, RECEIVERS), jnp.float32)
    return values * rising


def plant(entries, key, least, top_value):
    dims = entries.shape
    index_at = [jax.random.randint(jax.random.fold_in(key, axis), (), 0, dims[axis]) for axis in range(len(dims))]
    entries = entries.at[tuple(index_at)].set(least)
    longest = dims.index(max(dims))
    index_at[longest] = (index_at[longest] + 1) % dims[longest]
    return entries.at[tuple(index_at)].set(top_value)


def steps_of(stream_key, shape, shards, least, top_value):
    level = 1.0
    for dim, blocks in shards:
        steps = jax.random.uniform(jax.random.fold_in(jax.random.fold_in(stream_key, 6), dim), (blocks,), jnp.float32, least / len(shards), top_value / len(shards))
        level = level * jnp.repeat(jnp.exp(steps), shape[dim] // blocks).reshape((-1,) + (1,) * (len(shape) - 1 - dim))
    return level


def scatter_about(rng, extent, deviation, bound, split=(), kind=jnp.bfloat16):
    gain = steps_of(rng, extent, split, -0.22, 0.18) if split else 1.0
    entries = jax.random.normal(rng, extent, jnp.float32) * deviation * gain
    return jnp.minimum(jnp.maximum(entries, -bound), bound).astype(kind)


def setup_inputs(seed: int = 0) -> dict:
    key_list = jax.random.split(jax.random.key(seed), 9)
    state_now = scatter_about(key_list[0], (EVENTS, NX, NY, NZ), 1.0, 6.0, ((0, 4), (1, 8)), jnp.float32)
    state_prev = scatter_about(key_list[1], (EVENTS, NX, NY, NZ), 1.0, 6.0, ((0, 4), (1, 8)), jnp.float32)
    adjoint_now = scatter_about(key_list[2], (EVENTS, NX, NY, NZ), 0.3, 1.8, ((0, 4), (1, 8)), jnp.float32)
    adjoint_next = scatter_about(key_list[3], (EVENTS, NX, NY, NZ), 0.3, 1.8, ((0, 4), (1, 8)), jnp.float32)
    modulus = jnp.clip(jnp.exp(math.log(2.0) - 1.3862944 * jax.random.uniform(key_list[4], (NODES_1D, EX, NODES_1D, EY, NODES_1D, EZ), jnp.float32) ** steps_of(key_list[4], (NODES_1D, EX, NODES_1D, EY, NODES_1D, EZ), ((1, 8),), -0.2, 0.2)), 0.5, 2.0)
    density = jnp.clip(jnp.exp(math.log(2.0) - 1.3862944 * jax.random.uniform(key_list[5], (NX, NY, NZ), jnp.float32) ** steps_of(key_list[5], (NX, NY, NZ), ((0, 8),), -0.2, 0.2)), 0.5, 2.0)
    receivers = plant(jax.random.randint(key_list[6], (RECEIVERS,), 0, NODES_DEV), jax.random.fold_in(key_list[6], 1), 0, NODES_DEV - 1).astype(jnp.int32)
    observed = draw_observed(jax.random.fold_in(key_list[8], 71), 0)
    return {"state_now": state_now, "state_prev": state_prev, "adjoint_now": adjoint_now, "adjoint_next": adjoint_next, "modulus": modulus, "density": density, "receivers": receivers, "observed": observed}


TIME_STEP = 0.05
EPSILON = 1e-06

def gll_tables():
    root = math.sqrt(3.0 / 7.0)
    points = np.array([-1.0, -root, 0.0, root, 1.0])
    weights = np.array([0.1, 49.0 / 90.0, 32.0 / 45.0, 49.0 / 90.0, 0.1])
    legendre = (35.0 * points ** 4 - 30.0 * points ** 2 + 3.0) / 8.0
    derivative = np.zeros((5, 5))
    for row in range(5):
        for column in range(5):
            if row != column:
                derivative[row, column] = legendre[row] / (legendre[column] * (points[row] - points[column]))
    derivative[0, 0] = -5.0
    derivative[4, 4] = 5.0
    return (jnp.asarray(derivative, dtype=jnp.float32), jnp.asarray(weights, dtype=jnp.float32))

def cube_of(weights):
    return weights[:, None, None, None, None, None] * weights[None, None, :, None, None, None] * weights[None, None, None, None, :, None]

def line_weights(length, first_index):
    indices = first_index + jnp.arange(length, dtype=jnp.int32)
    position = indices % 4
    values = jnp.where(position == 1, 49.0 / 90.0, jnp.where(position == 2, 32.0 / 45.0, jnp.where(position == 3, 49.0 / 90.0, 0.2)))
    return jnp.where(indices == 0, 0.1, values).astype(jnp.float32)

def split_axis(field, axis_at, elements):
    pieces = [lax.slice_in_dim(field, offset, offset + 4 * (elements - 1) + 1, stride=4, axis=axis_at) for offset in range(5)]
    return jnp.stack(pieces, axis=axis_at)

def merge_axis(blocks, axis_at, elements):
    pieces = [lax.index_in_dim(blocks, offset, axis_at, keepdims=False) for offset in range(5)]
    zero_part = jnp.zeros_like(pieces[4])
    new_shape = pieces[0].shape[:axis_at] + (4 * elements,) + pieces[0].shape[axis_at + 1:]
    leading = jnp.stack(pieces[:4], axis=axis_at + 1).reshape(new_shape)
    trailing = jnp.stack([pieces[4], zero_part, zero_part, zero_part], axis=axis_at + 1).reshape(new_shape)
    pad_lead = [(0, 0)] * len(new_shape)
    pad_rear = [(0, 0)] * len(new_shape)
    pad_lead[axis_at] = (0, 1)
    pad_rear[axis_at] = (4, 0)
    leading = jnp.pad(leading, pad_lead)
    trailing = lax.slice_in_dim(jnp.pad(trailing, pad_rear), 0, 4 * elements + 1, axis=axis_at)
    return leading + trailing

def to_elements(nodes, count_x, count_y, count_z):
    blocks = split_axis(nodes, 2, count_z)
    blocks = split_axis(blocks, 1, count_y)
    return split_axis(blocks, 0, count_x)

def to_nodes(blocks, count_x, count_y, count_z):
    nodes = merge_axis(blocks, 0, count_x)
    nodes = merge_axis(nodes, 1, count_y)
    return merge_axis(nodes, 2, count_z)

def gradients_of(blocks, derivative):
    highest = lax.Precision.HIGHEST
    grad_x = jnp.einsum('sp,piqjrl->siqjrl', derivative, blocks, precision=highest)
    grad_y = jnp.einsum('sq,piqjrl->pisjrl', derivative, blocks, precision=highest)
    grad_z = jnp.einsum('sr,piqjrl->piqjsl', derivative, blocks, precision=highest)
    return (grad_x, grad_y, grad_z)

def element_force(blocks, element_stiff, derivative):
    highest = lax.Precision.HIGHEST
    grads = gradients_of(blocks, derivative)
    back = jnp.einsum('sp,siqjrl->piqjrl', derivative, element_stiff * grads[0], precision=highest)
    back = back + jnp.einsum('sq,pisjrl->piqjrl', derivative, element_stiff * grads[1], precision=highest)
    back = back + jnp.einsum('sr,piqjsl->piqjrl', derivative, element_stiff * grads[2], precision=highest)
    return (back, grads)

def inner_sum(first, second):
    return first[0] * second[0] + first[1] * second[1] + first[2] * second[2]

def reference(state_now, state_prev, adjoint_now, adjoint_next, modulus, density, receivers, observed):
    derivative, weights = gll_tables()
    weight_cube = cube_of(weights)
    element_stiff = weight_cube * modulus
    mass = density * line_weights(NX, 0)[:, None, None] * line_weights(NY, 0)[None, :, None] * line_weights(NZ, 0)[None, None, :]
    update_scale = TIME_STEP * TIME_STEP / mass
    owner = jnp.arange(RECEIVERS, dtype=jnp.int32) // REC_DEV
    plane_size = NY * NZ
    global_node = ((owner * (4 * EXD) + receivers // plane_size) * plane_size + receivers % plane_size).astype(jnp.int32)

    def global_blocks(nodal):
        return to_elements(jnp.pad(nodal, ((0, 1), (0, 1), (0, 1))), EX, EY, EZ)

    def global_force(nodal):
        forces, grads = element_force(global_blocks(nodal), element_stiff, derivative)
        return (to_nodes(forces, EX, EY, EZ)[:NX, :NY, :NZ], grads)

    def one_event(inputs):
        start_now, start_prev, adjoint_start, adjoint_after, observed_event = inputs

        def forward_step(state, unused):
            previous, current = state
            node_force, unused_grads = global_force(current)
            following = 2.0 * current - previous - update_scale * node_force
            return ((current, following), (current, following.reshape(-1)[global_node]))
        unused_state, (snapshots, records) = lax.scan(forward_step, (start_prev, start_now), None, length=NT)
        residual = records - observed_event
        energy = jnp.sum(observed_event * observed_event)
        misfit_sum = jnp.sum(residual * residual)
        mean_square = energy / (NT * RECEIVERS) + EPSILON
        misfit = 0.5 * misfit_sum / (NT * RECEIVERS * mean_square)
        sources = residual / mean_square

        def adjoint_step(state, inputs_step):
            adjoint_following, adjoint_current, accumulated = state
            snapshot, source = inputs_step
            node_force, adjoint_grads = global_force(adjoint_current)
            forward_grads = gradients_of(global_blocks(snapshot), derivative)
            accumulated = accumulated + inner_sum(forward_grads, adjoint_grads)
            injected = jnp.zeros((NX * NY * NZ,), jnp.float32).at[global_node].add(source).reshape(NX, NY, NZ)
            preceding = 2.0 * adjoint_current - adjoint_following + update_scale * (injected - node_force)
            return ((adjoint_current, preceding, accumulated), None)
        zero_total = jnp.zeros((5, EX, 5, EY, 5, EZ), jnp.float32)
        (unused_next, adjoint_last, accumulated), unused_out = lax.scan(adjoint_step, (adjoint_after, adjoint_start, zero_total), (snapshots[1:][::-1], sources[:NT - 1][::-1]))
        accumulated = accumulated + inner_sum(gradients_of(global_blocks(snapshots[0]), derivative), gradients_of(global_blocks(adjoint_last), derivative))
        return (-weight_cube * accumulated, misfit)
    kernels, misfits = lax.map(one_event, (state_now, state_prev, adjoint_now, adjoint_next, observed))
    summed = lax.optimization_barrier(jnp.sum(kernels, axis=0))
    largest = jnp.max(jnp.abs(summed))
    return (summed / (largest + EPSILON), misfits)
```

```python
import math

import jax
import jax.numpy as jnp
import ml_dtypes
import numpy as np
from jax import lax
from jax.experimental import pallas as pl
from jax.experimental.pallas import tpu as pltpu
from jax.sharding import PartitionSpec as P

TIME_STEP = 0.05
EPSILON = 1e-06
F32 = jnp.float32
BF16 = jnp.bfloat16


def gll_tables():
    root = math.sqrt(3.0 / 7.0)
    points = np.array([-1.0, -root, 0.0, root, 1.0])
    weights = np.array([0.1, 49.0 / 90.0, 32.0 / 45.0, 49.0 / 90.0, 0.1])
    legendre = (35.0 * points**4 - 30.0 * points**2 + 3.0) / 8.0
    derivative = np.zeros((5, 5))
    for row in range(5):
        for column in range(5):
            if row != column:
                derivative[row, column] = legendre[row] / (
                    legendre[column] * (points[row] - points[column])
                )
    derivative[0, 0] = -5.0
    derivative[4, 4] = 5.0
    return derivative, weights


DERIVATIVE, WEIGHTS = gll_tables()
LINE = [0.2, 49.0 / 90.0, 32.0 / 45.0, 49.0 / 90.0]


def apply_line(matrix, v):
    m = matrix
    o0, o1 = v[0] - v[4], v[1] - v[3]
    e0, e1 = v[0] + v[4], v[1] + v[3]
    out = [None] * 5
    for s in (0, 1):
        odd = float((m[s, 0] - m[s, 4]) / 2) * o0 + float((m[s, 1] - m[s, 3]) / 2) * o1
        even = (
            float((m[s, 0] + m[s, 4]) / 2) * e0
            + float((m[s, 1] + m[s, 3]) / 2) * e1
            + float(m[s, 2]) * v[2]
        )
        out[s], out[4 - s] = odd + even, odd - even
    out[2] = float(m[2, 0]) * o0 + float(m[2, 1]) * o1
    return out


def thirds(x):
    high = x.astype(BF16)
    rest = x - high.astype(F32)
    mid = rest.astype(BF16)
    return high, mid, (rest - mid.astype(F32)).astype(BF16)


def dot(a, b):
    return jnp.dot(a, b, preferred_element_type=F32)


def dot_rows(a, b):
    return lax.dot_general(a, b, (((1,), (1,)), ((), ())), preferred_element_type=F32)


def tables(ex, ey, ez, fields):
    ny, nz = 4 * ey, 4 * ez
    column = np.zeros((nz, nz), np.float32)
    for r in range(4):
        for l in range(ez):
            column[4 * l + r, r * ez + l] = 1
    rows = np.zeros((4 * ex * ny, 4 * ex * ny), np.float32)
    plane = np.zeros((fields * 32, fields * ny), np.float32)
    for q in range(4):
        for j in range(ey):
            for i in range(ex):
                for p in range(4):
                    rows[(p * 4 + q) * 8 + i * ey + j, (i * 4 + p) * ny + j * 4 + q] = 1
            for f in range(fields):
                plane[f * 32 + q * 8 + (ex - 1) * ey + j, f * ny + j * 4 + q] = 1
    cube = np.zeros((128, ez), np.float32)
    w = WEIGHTS
    cube[:125] = -(w[:, None, None] * w[None, :, None] * w[None, None, :]).reshape(125, 1)
    as_bf16 = [t.astype(ml_dtypes.bfloat16) for t in (column, rows, plane)]
    return as_bf16 + [cube]


def make_kernel(ex, ey, ez, steps, events, spaces, receivers_total):
    ny, nz = 4 * ey, 4 * ez
    half = (ex - 1) * ey
    shift_y = int(math.log2(nz))
    shift_x = shift_y + int(math.log2(ny))
    shift_j = int(math.log2(ey))
    last = steps - 1
    samples = steps * receivers_total

    def kernel(
        now_ref, prev_ref, adj_ref, next_ref, density_ref, modulus_ref, rec_ref, obs_ref,
        column_ref, rows_ref, plane_ref, cube_ref,
        out_ref, misfit_ref,
        halo, halo_rec, halo_obs, u, lam, before, scale, stiff, grads, force, total, inject,
        row_mask, lane_mask, row_mask_h, lane_mask_h,
        send_l, send_r, recv_l, recv_r, sums_out, sums_in, pack, got, relay, tops_out, tops_in, tops_far,
        final,
        halo_ss, halo_rs, ls, lr, rs, rr, sum_s, sum_r, red_s, red_r, top_s, top_r, far_s, far_r,
    ):
        me = lax.axis_index("space")
        event = lax.axis_index("event")
        left = jnp.maximum(me - 1, 0)
        right = jnp.minimum(me + 1, spaces - 1)
        has_left, has_right = me > 0, me < spaces - 1
        MESH = pl.DeviceIdType.MESH

        barrier = pltpu.get_barrier_semaphore()

        @pl.loop(1, spaces)
        def _(k):
            pl.semaphore_signal(
                barrier, inc=1, device_id={"space": lax.rem(me + k, spaces)}, device_id_type=MESH
            )

        for k in range(1, events):
            pl.semaphore_signal(
                barrier, inc=1, device_id={"event": lax.rem(event + k, events)}, device_id_type=MESH
            )

        @pl.when(jnp.logical_not(has_right))
        def _():
            halo[0:4] = jnp.zeros((4, ny, nz), F32)
            halo[4] = jnp.ones((ny, nz), F32)
            halo_rec[...] = jnp.zeros_like(halo_rec)
            halo_obs[...] = jnp.zeros_like(halo_obs)
            recv_r[...] = jnp.zeros_like(recv_r)

        @pl.when(jnp.logical_not(has_left))
        def _():
            recv_l[...] = jnp.zeros_like(recv_l)

        pl.semaphore_wait(barrier, spaces - 1 + events - 1)

        def to_left(src, dst, ss, sr):
            return pltpu.make_async_remote_copy(
                src_ref=src, dst_ref=dst, send_sem=ss, recv_sem=sr,
                device_id={"space": left}, device_id_type=MESH,
            )

        def to_right(src, dst, ss, sr):
            return pltpu.make_async_remote_copy(
                src_ref=src, dst_ref=dst, send_sem=ss, recv_sem=sr,
                device_id={"space": right}, device_id_type=MESH,
            )

        own = (now_ref, prev_ref, adj_ref, next_ref, density_ref)
        planes = [r.at[0, 0] for r in own[:4]] + [density_ref.at[0]]
        halo_copies = [
            to_left(planes[f], halo.at[f], halo_ss.at[f], halo_rs.at[f]) for f in range(5)
        ]
        halo_copies.append(to_left(rec_ref, halo_rec, halo_ss.at[5], halo_rs.at[5]))
        halo_copies.append(to_left(obs_ref.at[0], halo_obs, halo_ss.at[6], halo_rs.at[6]))

        @pl.when(has_left)
        def _():
            for copy in halo_copies:
                copy.start()

        def share(slot, k):
            there = lax.rem(me + k, spaces)
            return pltpu.make_async_remote_copy(
                src_ref=sums_out.at[slot], dst_ref=sums_in.at[slot, me],
                send_sem=sum_s.at[slot, k], recv_sem=sum_r.at[slot, me],
                device_id={"space": there}, device_id_type=MESH,
            )

        def taken(slot, k):
            there = lax.rem(me + k, spaces)
            return pltpu.make_async_remote_copy(
                src_ref=sums_out.at[slot], dst_ref=sums_in.at[slot, there],
                send_sem=sum_s.at[slot, k], recv_sem=sum_r.at[slot, there],
                device_id={"space": there}, device_id_type=MESH,
            )

        def share_all(slot, lanes):
            tile = jnp.broadcast_to(lanes, (8, lanes.shape[1]))
            sums_out[slot] = tile
            sums_in[slot, me] = tile

            @pl.loop(1, spaces)
            def _(k):
                share(slot, k).start()

        def take_all(slot):
            @pl.loop(1, spaces)
            def _(k):
                copy = taken(slot, k)
                copy.wait_send()
                copy.wait_recv()

            tile = jnp.sum(sums_in[slot], axis=0)
            return jnp.sum(tile[0:1, :], axis=1, keepdims=True)

        observed = obs_ref[0]
        share_all(0, jnp.sum(observed * observed, axis=0, keepdims=True))

        def iota(shape, axis):
            return lax.broadcasted_iota(jnp.int32, shape, axis)

        def store_nodes(dst, f, rows, values):
            for r in range(4):
                part = values[:, r * ez : (r + 1) * ez]
                dst(f, r, part.reshape(rows + (8, ez)))

        def put(f, r, value):
            if f == 0:
                u[0, 0:4, 0:4, r] = value
            elif f == 1:
                before[0, 0:4, :, r] = value
            elif f == 2:
                lam[0, 0:4, 0:4, r] = value
            elif f == 3:
                before[1, 0:4, :, r] = value
            else:
                scale[0:4, :, r] = value

        def put_plane(f, r, value):
            if f == 0:
                u[0, 4, 0:4, r] = value
            elif f == 1:
                before[0, 4, :, r] = value
            elif f == 2:
                lam[0, 4, 0:4, r] = value
            elif f == 3:
                before[1, 4, :, r] = value
            else:
                scale[4, :, r] = value

        for f in range(5):
            nodes = own[f][0] if f < 4 else own[f][...]
            nodes = nodes.reshape(4 * ex * ny, nz)
            parts = [dot(rows_ref[...], part).astype(BF16) for part in thirds(nodes)]
            parts = [dot(part, column_ref[...]) for part in parts]
            store_nodes(put, f, (4, 4), parts[0] + parts[1] + parts[2])

        flat = stiff.reshape(125 * 8, ez)
        at_r = iota((5, ez), 0)
        ends = jnp.logical_or(at_r == 0, at_r == 4)
        w_r = jnp.where(ends, WEIGHTS[0], jnp.where(at_r == 2, WEIGHTS[2], WEIGHTS[1])).astype(F32)
        for p in range(5):
            for q in range(5):
                w_pqr = w_r * float(WEIGHTS[p] * WEIGHTS[q])
                for i in range(ex):
                    for j in range(ey):
                        at = (p * 5 + q) * 40 + i * ey + j
                        flat[pl.ds(at, 5, stride=8), :] = modulus_ref[p, i, q, j] * w_pqr

        def masks(rec, rows_out, lanes_out, plane_only):
            x = lax.shift_right_logical(rec, shift_x)
            y = lax.shift_right_logical(rec, shift_y) & (ny - 1)
            z = rec & (nz - 1)
            p, i = x & 3, lax.shift_right_logical(x, 2)
            q, j = y & 3, lax.shift_right_logical(y, 2)
            r, l = z & 3, lax.shift_right_logical(z, 2)
            if plane_only:
                row = (q * 4 + r) * 8 + half + j
                row = jnp.where(x == 0, row, -1)
            else:
                row = ((p * 4 + q) * 4 + r) * 8 + i * ey + j
            shape = rows_out.shape
            rows_out[...] = jnp.where(iota(shape, 0) == jnp.broadcast_to(row, shape), 1.0, 0.0)
            shape = lanes_out.shape
            hit = jnp.where(iota(shape, 0) == jnp.broadcast_to(l, shape), 1.0, 0.0)
            lanes_out[...] = hit.astype(BF16)

        masks(rec_ref[...], row_mask, lane_mask, False)

        @pl.when(has_left)
        def _():
            for copy in halo_copies:
                copy.wait_send()

        @pl.when(has_right)
        def _():
            for copy in halo_copies:
                copy.wait_recv()

        masks(halo_rec[...], row_mask_h, lane_mask_h, True)
        nodes = halo[...].reshape(5 * ny, nz)
        parts = [dot(plane_ref[...], part).astype(BF16) for part in thirds(nodes)]
        parts = [dot(part, column_ref[...]) for part in parts]
        summed = parts[0] + parts[1] + parts[2]
        for f in range(5):
            store_nodes(put_plane, f, (4,), summed[f * 32 : (f + 1) * 32])

        row8, lane8 = iota((8, ez), 0), iota((8, ez), 1)
        first_x = jnp.logical_and(row8 < ey, me == 0)
        half_x = jnp.where(first_x, 0.5, 1.0).astype(F32)
        half_y = jnp.where((row8 & (ey - 1)) == 0, 0.5, 1.0).astype(F32)
        half_z = jnp.where(lane8 == 0, 0.5, 1.0).astype(F32)
        kept = jnp.where(jnp.logical_and(row8 >= half, has_right), 1.0, 0.0).astype(F32)
        for p in range(5):
            for q in range(4):
                for r in range(4):
                    weight = float(LINE[p % 4] * LINE[q] * LINE[r])
                    mass = scale[p, q, r] * weight if p < 4 else jnp.where(
                        row8 >= half, scale[p, q, r], 1.0) * weight
                    if p == 0:
                        mass = mass * half_x
                    if q == 0:
                        mass = mass * half_y
                    if r == 0:
                        mass = mass * half_z
                    value = (TIME_STEP * TIME_STEP) / mass
                    scale[p, q, r] = value * kept if p == 4 else value

        def turn(x, by, axis):
            shape = x.shape
            flat_x = x.reshape((-1,) + shape[-2:])
            pieces = [
                pltpu.roll(flat_x[n], by % shape[axis], axis + 2)[None] for n in range(flat_x.shape[0])
            ]
            return jnp.concatenate(pieces, axis=0).reshape(shape)

        def low(shape):
            return iota(shape, len(shape) - 2) < half

        def fill(e):
            shape = (4, 4, 8, ez)
            e[4, 0:4, 0:4] = jnp.where(
                low(shape), turn(e[0, 0:4, 0:4], -ey, -2), e[4, 0:4, 0:4]
            )
            shape = (5, 4, 8, ez)
            inner = (iota(shape, 2) & (ey - 1)) != ey - 1
            e[:, 4, 0:4] = jnp.where(inner, turn(e[:, 0, 0:4], -1, -2), 0.0)
            shape = (5, 5, 8, ez)
            e[:, :, 4] = jnp.where(iota(shape, 3) != ez - 1, turn(e[:, :, 0], -1, -1), 0.0)

        def stencil(e, f, store=None, partner=None, fresh=False):
            @pl.loop(0, 5)
            def _(q):
                g = apply_line(DERIVATIVE, [e[p, q] for p in range(5)])
                for p in range(5):
                    if store is not None:
                        store[0, p, q] = g[p]
                    if partner is not None:
                        product = g[p] * partner[0, p, q]
                        total[p, q] = product if fresh else total[p, q] + product
                if f is not None:
                    back = apply_line(DERIVATIVE.T, [stiff[p, q] * g[p] for p in range(5)])
                    for p in range(5):
                        f[p, q] = back[p]

            @pl.loop(0, 5)
            def _(p):
                g = apply_line(DERIVATIVE, [e[p, q] for q in range(5)])
                for q in range(5):
                    if store is not None:
                        store[1, p, q] = g[q]
                    if partner is not None:
                        total[p, q] = total[p, q] + g[q] * partner[1, p, q]
                if f is not None:
                    back = apply_line(DERIVATIVE.T, [stiff[p, q] * g[q] for q in range(5)])
                    for q in range(5):
                        f[p, q] = f[p, q] + back[q]
                g = apply_line(DERIVATIVE, [e[p, :, r] for r in range(5)])
                for r in range(5):
                    if store is not None:
                        store[2, p, :, r] = g[r]
                    if partner is not None:
                        total[p, :, r] = total[p, :, r] + g[r] * partner[2, p, :, r]
                if f is not None:
                    back = apply_line(DERIVATIVE.T, [stiff[p, :, r] * g[r] for r in range(5)])
                    for r in range(5):
                        f[p, :, r] = f[p, :, r] + back[r]

        def messages(m):
            return (
                to_left(send_l.at[m], recv_r.at[m], ls.at[m], lr.at[m]),
                to_right(send_r.at[m], recv_l.at[m], rs.at[m], rr.at[m]),
            )

        def assemble(f, m):
            shape = (5, 5, 8, ez)
            f[:, :, 0] = f[:, :, 0] + jnp.where(iota(shape, 3) != 0, turn(f[:, :, 4], 1, -1), 0.0)
            shape = (5, 4, 8, ez)
            inner = (iota(shape, 2) & (ey - 1)) != 0
            f[:, 0, 0:4] = f[:, 0, 0:4] + jnp.where(inner, turn(f[:, 4, 0:4], 1, -2), 0.0)
            pair = (2, 4, 8, ez)
            send_l[m] = jnp.where(low(pair), f[0, 0:2, 0:4], turn(f[0, 2:4, 0:4], half, -2))
            send_r[m] = jnp.where(low(pair), turn(f[4, 0:2, 0:4], half, -2), f[4, 2:4, 0:4])
            leftward, rightward = messages(m)

            @pl.when(has_left)
            def _():
                leftward.start()

            @pl.when(has_right)
            def _():
                rightward.start()

            shape = (4, 4, 8, ez)
            f[0, 0:4, 0:4] = f[0, 0:4, 0:4] + jnp.where(
                low(shape), 0.0, turn(f[4, 0:4, 0:4], ey, -2)
            )

        def receive(f, m):
            leftward, rightward = messages(m)

            @pl.when(has_left)
            def _():
                leftward.wait_send()
                rightward.wait_recv()

            @pl.when(has_right)
            def _():
                rightward.wait_send()
                leftward.wait_recv()

            pair = (2, 4, 8, ez)
            near = recv_l[m]
            f[0, 0:2, 0:4] = f[0, 0:2, 0:4] + jnp.where(low(pair), near, 0.0)
            f[0, 2:4, 0:4] = f[0, 2:4, 0:4] + jnp.where(low(pair), turn(near, half, -2), 0.0)
            far = recv_r[m]
            f[4, 0:2, 0:4] = f[4, 0:2, 0:4] + turn(far, half, -2)
            f[4, 2:4, 0:4] = f[4, 2:4, 0:4] + far

        def advance(new, current, old, f, count=5):
            for p in range(count):
                new[p, 0:4, 0:4] = (
                    2.0 * current[p, 0:4, 0:4]
                    - old[p, 0:4, 0:4]
                    - scale[p] * f[p, 0:4, 0:4]
                )

        def read(nodes, rows, lanes):
            x = sum(dot(part, lanes[...]) for part in thirds(nodes))
            return jnp.sum(x * rows[...], axis=0, keepdims=True)

        def spread(source, rows, lanes):
            x = rows[...]
            return sum(
                dot_rows((x * part.astype(F32)).astype(BF16), lanes[...]) for part in thirds(source)
            )

        def records(e):
            return read(e[0:4, 0:4, 0:4].reshape(64 * 8, ez), row_mask, lane_mask)

        def records_h(e):
            return read(e[4, 0:4, 0:4].reshape(16 * 8, ez), row_mask_h, lane_mask_h)

        fu, fl = force.at[0], force.at[1]
        residual_sum = None
        mean_square = None
        for n in range(steps):
            e = u.at[n]
            if n < last:
                if n == 0:
                    fill(e)
                stencil(e, fu, store=grads.at[n])
                assemble(fu, n)
                if n == 0:
                    fill(lam.at[0])
                    stencil(lam.at[0], fl, store=grads.at[last])
                    assemble(fl, steps)
                if n > 0:
                    residual, source, source_h = sources_of(u.at[n], n)
                receive(fu, n)
                advance(u.at[n + 1], e, before.at[0] if n == 0 else u.at[n - 1], fu)
                fill(u.at[n + 1])
            if n == 0:
                energy = take_all(0)
                mean_square = energy / samples + EPSILON

                def sources_of(e, n):
                    residual = records(e) - obs_ref[0, n - 1 : n, :]
                    residual_h = records_h(e) - halo_obs[n - 1 : n, :]
                    source, source_h = residual / mean_square, residual_h / mean_square
                    whole = spread(source, row_mask, lane_mask)
                    inject[n - 1, 0:4] = whole.reshape(4, 4, 4, 8, ez)
                    inject[n - 1, 4] = spread(source_h, row_mask_h, lane_mask_h).reshape(4, 4, 8, ez)
                    return residual, source, source_h

            if n > 0 and n < last:
                residual_sum = residual * residual if residual_sum is None else (
                    residual_sum + residual * residual
                )
        residual, _, _ = sources_of(u.at[last], last)
        residual_sum = residual * residual if residual_sum is None else (
            residual_sum + residual * residual
        )

        receive(fl, steps)
        for k, n in enumerate(range(last, 0, -1)):
            for p in range(5):
                fl[p, 0:4, 0:4] = fl[p, 0:4, 0:4] - inject[n - 1, p]
            advance(lam.at[k + 1], lam.at[k], before.at[1] if k == 0 else lam.at[k - 1], fl)
            fill(lam.at[k + 1])
            if n - 1 > 0:
                stencil(lam.at[k + 1], fl, partner=grads.at[n - 1], fresh=k == 0)
                assemble(fl, steps + 1 + k)
                if k == 0:
                    stencil(u.at[last], fu, partner=grads.at[last])
                    assemble(fu, last)
                receive(fl, steps + 1 + k)
        stencil(lam.at[last], None, partner=grads.at[0])

        flat_total = total.reshape(125 * 8, ez)
        beside = event + 1 - 2 * lax.rem(event, 2)
        across = lax.rem(event + 2, events)
        beyond = lax.rem(beside + 2, events)
        for owner in range(events):
            for i in range(ex):
                pack[owner, i, 120:128] = jnp.zeros((8, ez), F32)
                pack[owner, i, 0:125] = flat_total[pl.ds(i * ey + owner, 125, stride=8), :]

        def reduce_copy(src, slot, there):
            return pltpu.make_async_remote_copy(
                src_ref=src, dst_ref=got.at[slot], send_sem=red_s.at[slot], recv_sem=red_r.at[slot],
                device_id={"event": there}, device_id_type=MESH,
            )

        first = reduce_copy(pack.at[beyond], 0, beside)
        second = reduce_copy(pack.at[beside], 1, beside)
        first.start()
        second.start()
        first.wait()
        relay[...] = pack[across] + got[0]
        third = reduce_copy(relay, 2, across)
        third.start()

        receive(fu, last)
        u3 = u.at[steps]
        advance(u3, u.at[last], u.at[last - 1] if last > 0 else before.at[0], fu, count=4)
        residual = records(u3) - obs_ref[0, last : last + 1, :]
        share_all(1, residual_sum + residual * residual)

        second.wait()
        pair_sum = pack[event] + got[1]
        third.wait()
        cube = jnp.broadcast_to(cube_ref[...][None], (ex, 128, ez))
        value = (pair_sum + got[2]) * cube
        final[...] = value

        top = jnp.max(jnp.abs(value).reshape(ex * 16, 8, ez), axis=0)
        tops_out[0] = top
        tops_in[event] = top
        for k in range(1, events):
            pltpu.make_async_remote_copy(
                src_ref=tops_out.at[0], dst_ref=tops_in.at[event],
                send_sem=top_s.at[k], recv_sem=top_r.at[event],
                device_id={"event": lax.rem(event + k, events)}, device_id_type=MESH,
            ).start()
        for k in range(1, events):
            there = lax.rem(event + k, events)
            copy = pltpu.make_async_remote_copy(
                src_ref=tops_out.at[0], dst_ref=tops_in.at[there],
                send_sem=top_s.at[k], recv_sem=top_r.at[there],
                device_id={"event": there}, device_id_type=MESH,
            )
            copy.wait_send()
            copy.wait_recv()
        top = jnp.max(tops_in[...], axis=0)
        tops_out[1] = top
        tops_far[me] = top

        @pl.loop(1, spaces)
        def _(k):
            pltpu.make_async_remote_copy(
                src_ref=tops_out.at[1], dst_ref=tops_far.at[me],
                send_sem=far_s.at[k], recv_sem=far_r.at[me],
                device_id={"space": lax.rem(me + k, spaces)}, device_id_type=MESH,
            ).start()

        misfit_sum = take_all(1)
        misfit_ref[...] = jnp.broadcast_to(
            0.5 * misfit_sum / (samples * mean_square), misfit_ref.shape
        )

        @pl.loop(1, spaces)
        def _(k):
            there = lax.rem(me + k, spaces)
            copy = pltpu.make_async_remote_copy(
                src_ref=tops_out.at[1], dst_ref=tops_far.at[there],
                send_sem=far_s.at[k], recv_sem=far_r.at[there],
                device_id={"space": there}, device_id_type=MESH,
            )
            copy.wait_send()
            copy.wait_recv()

        top = jnp.max(tops_far[...], axis=0)
        top = jnp.max(jnp.max(top, axis=1, keepdims=True), axis=0, keepdims=True)
        inverse = 1.0 / (top + EPSILON)
        final[...] = final[...] * inverse[None]
        for p in range(5):
            for i in range(ex):
                for q in range(5):
                    at = (p * 5 + q) * 5
                    out_ref[p, i, q, 0] = final[i, at : at + 5, :]

    return kernel


def shards(mesh_shape, now, prev, adj, nxt, modulus, density, receivers, observed):
    events, spaces = mesh_shape["event"], mesh_shape["space"]
    ex, ey, ez = modulus.shape[1], modulus.shape[3], modulus.shape[5]
    steps, count = observed.shape[1], receivers.shape[0]
    assert ex * ey == 8 and ex == 2 and ez == 128 and count == 128 and events == 4 == ey
    assert steps >= 3 and now.shape[0] == 1
    ny, nz = now.shape[2], now.shape[3]
    column, rows, plane, cube = tables(ex, ey, ez, 5)
    kernel = make_kernel(ex, ey, ez, steps, events, spaces, count * spaces)
    vm = lambda *shape: pltpu.VMEM(shape, F32)
    dma = lambda *shape: pltpu.SemaphoreType.DMA(shape)
    rounds = 2 * steps
    scratch = [
        vm(5, ny, nz), pltpu.VMEM((1, count), jnp.int32), vm(steps, count),
        vm(steps + 1, 5, 5, 5, 8, ez), vm(steps, 5, 5, 5, 8, ez), vm(2, 5, 4, 4, 8, ez),
        vm(5, 4, 4, 8, ez), vm(5, 5, 5, 8, ez), vm(steps, 3, 5, 5, 5, 8, ez),
        vm(2, 5, 5, 5, 8, ez), vm(5, 5, 5, 8, ez), vm(steps - 1, 5, 4, 4, 8, ez),
        vm(512, count), pltpu.VMEM((ez, count), BF16), vm(128, count),
        pltpu.VMEM((ez, count), BF16),
        vm(rounds, 2, 4, 8, ez), vm(rounds, 2, 4, 8, ez),
        vm(rounds, 2, 4, 8, ez), vm(rounds, 2, 4, 8, ez),
        vm(2, 8, ez), vm(2, spaces, 8, ez), vm(events, ex, 128, ez), vm(3, ex, 128, ez),
        vm(ex, 128, ez), vm(2, 8, ez), vm(events, 8, ez), vm(spaces, 8, ez), vm(ex, 128, ez),
        dma(7), dma(7), dma(rounds), dma(rounds), dma(rounds), dma(rounds),
        dma(2, spaces), dma(2, spaces), dma(3), dma(3),
        dma(events), dma(events), dma(spaces), dma(spaces),
    ]
    vmem = pl.BlockSpec(memory_space=pltpu.VMEM)
    out, misfit = pl.pallas_call(
        kernel,
        out_shape=(
            jax.ShapeDtypeStruct((5, ex, 5, ey // events, 5, ez), F32),
            jax.ShapeDtypeStruct((1, ez), F32),
        ),
        in_specs=[vmem] * 12,
        out_specs=(vmem, vmem),
        scratch_shapes=scratch,
        compiler_params=pltpu.CompilerParams(
            collective_id=0, has_side_effects=True, vmem_limit_bytes=48 * 1024 * 1024
        ),
        name="window",
    )(
        now, prev, adj, nxt, density, modulus, receivers.reshape(1, count), observed,
        jnp.asarray(column), jnp.asarray(rows), jnp.asarray(plane), jnp.asarray(cube),
    )
    return out, misfit[0, :1]


def solution(mesh):
    in_specs = (
        P("event", "space", None, None),
        P("event", "space", None, None),
        P("event", "space", None, None),
        P("event", "space", None, None),
        P(None, "space", None, None, None, None),
        P("space", None, None),
        P("space"),
        P("event", None, "space"),
    )
    out_specs = (P(None, "space", None, "event", None, None), P("event"))
    sizes = dict(mesh.shape)

    def program(*args):
        return shards(sizes, *args)

    return jax.shard_map(program, mesh=mesh, in_specs=in_specs, out_specs=out_specs, check_vma=False)
```

```python
import math

import jax
import jax.numpy as jnp
import ml_dtypes
import numpy as np
from jax import lax
from jax.experimental import pallas as pl
from jax.experimental.pallas import tpu as pltpu
from jax.sharding import PartitionSpec as P

TIME_STEP = 0.05
EPSILON = 1e-06
LIMIT = 64 * 1024 * 1024 - 128 * 1024
F32 = jnp.float32
BF16 = jnp.bfloat16


def gll_tables():
    root = math.sqrt(3.0 / 7.0)
    points = np.array([-1.0, -root, 0.0, root, 1.0])
    weights = np.array([0.1, 49.0 / 90.0, 32.0 / 45.0, 49.0 / 90.0, 0.1])
    legendre = (35.0 * points**4 - 30.0 * points**2 + 3.0) / 8.0
    derivative = np.zeros((5, 5))
    for row in range(5):
        for column in range(5):
            if row != column:
                derivative[row, column] = legendre[row] / (
                    legendre[column] * (points[row] - points[column])
                )
    derivative[0, 0] = -5.0
    derivative[4, 4] = 5.0
    return derivative, weights


DERIVATIVE, WEIGHTS = gll_tables()
LINE = [0.2, 49.0 / 90.0, 32.0 / 45.0, 49.0 / 90.0]


def apply_line(matrix, v):
    m = matrix
    o0, o1 = v[0] - v[4], v[1] - v[3]
    e0, e1 = v[0] + v[4], v[1] + v[3]
    out = [None] * 5
    for s in (0, 1):
        odd = float((m[s, 0] - m[s, 4]) / 2) * o0 + float((m[s, 1] - m[s, 3]) / 2) * o1
        even = (
            float((m[s, 0] + m[s, 4]) / 2) * e0
            + float((m[s, 1] + m[s, 3]) / 2) * e1
            + float(m[s, 2]) * v[2]
        )
        out[s], out[4 - s] = odd + even, odd - even
    out[2] = float(m[2, 0]) * o0 + float(m[2, 1]) * o1
    return out


def thirds(x):
    high = x.astype(BF16)
    rest = x - high.astype(F32)
    mid = rest.astype(BF16)
    return high, mid, (rest - mid.astype(F32)).astype(BF16)


def dot(a, b):
    return jnp.dot(a, b, preferred_element_type=F32)


def dot_rows(a, b):
    return lax.dot_general(a, b, (((1,), (1,)), ((), ())), preferred_element_type=F32)


def tables(ex, ey, ez):
    ny, nz = 4 * ey, 4 * ez
    column = np.zeros((nz, nz), np.float32)
    for r in range(4):
        for l in range(ez):
            column[4 * l + r, r * ez + l] = 1
    rows = np.zeros((4 * ex * ny, 4 * ex * ny), np.float32)
    plane = np.zeros((32, ny), np.float32)
    for q in range(4):
        for j in range(ey):
            for i in range(ex):
                for p in range(4):
                    rows[(p * 4 + q) * 8 + i * ey + j, (i * 4 + p) * ny + j * 4 + q] = 1
            plane[q * 8 + (ex - 1) * ey + j, j * 4 + q] = 1
    cube = np.zeros((128, ez), np.float32)
    w = WEIGHTS
    cube[:125] = -(w[:, None, None] * w[None, :, None] * w[None, None, :]).reshape(125, 1)
    as_bf16 = [t.astype(ml_dtypes.bfloat16) for t in (column, rows, plane)]
    return as_bf16 + [cube]


def make_kernel(ex, ey, ez, steps, events, spaces, receivers_total):
    ny, nz = 4 * ey, 4 * ez
    half = (ex - 1) * ey
    shift_y = int(math.log2(nz))
    shift_x = shift_y + int(math.log2(ny))
    shift_j = int(math.log2(ey))
    last = steps - 1
    samples = steps * receivers_total

    def kernel(
        now_hbm, prev_hbm, adj_hbm, next_hbm, density_hbm, modulus_hbm, rec_hbm, obs_hbm,
        column_hbm, rows_hbm, plane_hbm, cube_hbm,
        out_ref, misfit_ref,
        fields, modulus_ref, rec_ref, obs_ref, column_ref, rows_ref, plane_ref, cube_ref, in_sem,
        halo, halo_rec, halo_obs, u, lam, before, scale, stiff, grads, force, total, inject,
        row_mask, lane_mask, row_mask_h, lane_mask_h,
        send_l, send_r, recv_l, recv_r, sums_out, sums_in, pack, got, relay, tops_out, tops_in, tops_far,
        final,
        halo_ss, halo_rs, ls, lr, rs, rr, sum_s, sum_r, red_s, red_r, top_s, top_r, far_s, far_r,
    ):
        me = lax.axis_index("space")
        event = lax.axis_index("event")
        left = jnp.maximum(me - 1, 0)
        right = jnp.minimum(me + 1, spaces - 1)
        has_left, has_right = me > 0, me < spaces - 1
        MESH = pl.DeviceIdType.MESH

        own = [r.at[0] for r in (now_hbm, adj_hbm, prev_hbm, next_hbm)] + [density_hbm]
        local = [(own[0], fields.at[0]), (rows_hbm, rows_ref), (column_hbm, column_ref)]
        local += [(plane_hbm, plane_ref), (own[1], fields.at[1]), (modulus_hbm, modulus_ref)]
        local += [(own[f], fields.at[f]) for f in (2, 3, 4)]
        local += [(rec_hbm, rec_ref), (obs_hbm, obs_ref), (cube_hbm, cube_ref)]
        local = [
            pltpu.make_async_copy(src, dst, in_sem.at[k]) for k, (src, dst) in enumerate(local)
        ]

        barrier = pltpu.get_barrier_semaphore()

        @pl.loop(1, spaces)
        def _(k):
            pl.semaphore_signal(
                barrier, inc=1, device_id={"space": lax.rem(me + k, spaces)}, device_id_type=MESH
            )

        for k in range(1, events):
            pl.semaphore_signal(
                barrier, inc=1, device_id={"event": lax.rem(event + k, events)}, device_id_type=MESH
            )

        for copy in local:
            copy.start()

        @pl.when(jnp.logical_not(has_right))
        def _():
            halo[0:4] = jnp.zeros((4, ny, nz), F32)
            halo[4] = jnp.ones((ny, nz), F32)
            halo_rec[...] = jnp.zeros_like(halo_rec)
            halo_obs[...] = jnp.zeros_like(halo_obs)
            recv_r[...] = jnp.zeros_like(recv_r)

        @pl.when(jnp.logical_not(has_left))
        def _():
            recv_l[...] = jnp.zeros_like(recv_l)

        pl.semaphore_wait(barrier, spaces - 1 + events - 1)

        def to_left(src, dst, ss, sr):
            return pltpu.make_async_remote_copy(
                src_ref=src, dst_ref=dst, send_sem=ss, recv_sem=sr,
                device_id={"space": left}, device_id_type=MESH,
            )

        def to_right(src, dst, ss, sr):
            return pltpu.make_async_remote_copy(
                src_ref=src, dst_ref=dst, send_sem=ss, recv_sem=sr,
                device_id={"space": right}, device_id_type=MESH,
            )

        halo_copies = [
            to_left(own[f].at[0], halo.at[f], halo_ss.at[f], halo_rs.at[f]) for f in range(5)
        ]
        halo_copies.append(to_left(rec_hbm, halo_rec, halo_ss.at[5], halo_rs.at[5]))
        halo_copies.append(to_left(obs_hbm, halo_obs, halo_ss.at[6], halo_rs.at[6]))

        @pl.when(has_left)
        def _():
            for copy in halo_copies:
                copy.start()

        def halo_wait(numbers):
            @pl.when(has_right)
            def _():
                for k in numbers:
                    halo_copies[k].wait_recv()

        def share(slot, k):
            there = lax.rem(me + k, spaces)
            return pltpu.make_async_remote_copy(
                src_ref=sums_out.at[slot], dst_ref=sums_in.at[slot, me],
                send_sem=sum_s.at[slot, k], recv_sem=sum_r.at[slot, me],
                device_id={"space": there}, device_id_type=MESH,
            )

        def taken(slot, k):
            there = lax.rem(me + k, spaces)
            return pltpu.make_async_remote_copy(
                src_ref=sums_out.at[slot], dst_ref=sums_in.at[slot, there],
                send_sem=sum_s.at[slot, k], recv_sem=sum_r.at[slot, there],
                device_id={"space": there}, device_id_type=MESH,
            )

        def share_all(slot, lanes):
            tile = jnp.broadcast_to(lanes, (8, lanes.shape[1]))
            sums_out[slot] = tile
            sums_in[slot, me] = tile

            @pl.loop(1, spaces)
            def _(k):
                share(slot, k).start()

        def take_all(slot):
            @pl.loop(1, spaces)
            def _(k):
                copy = taken(slot, k)
                copy.wait_send()
                copy.wait_recv()

            tile = jnp.sum(sums_in[slot], axis=0)
            return jnp.sum(tile[0:1, :], axis=1, keepdims=True)

        def iota(shape, axis):
            return lax.broadcasted_iota(jnp.int32, shape, axis)

        def target(f):
            if f < 2:
                return (u, lam)[f].at[0]
            return before.at[f - 2] if f < 4 else scale

        def order(nodes, rows):
            count = rows.shape[0]
            parts = [dot(rows[...], part).astype(BF16) for part in thirds(nodes)]
            x = dot(jnp.concatenate(parts, axis=0), column_ref[...])
            return x[:count] + x[count : 2 * count] + x[2 * count :]

        def order_own(f):
            values = order(fields[f].reshape(4 * ex * ny, nz), rows_ref)
            for r in range(4):
                part = values[:, r * ez : (r + 1) * ez]
                target(f)[0:4, 0:4, r] = part.reshape(4, 4, 8, ez)

        def order_halo(f):
            values = order(halo[f], plane_ref)
            for r in range(4):
                part = values[:, r * ez : (r + 1) * ez]
                target(f)[4, 0:4, r] = part.reshape(4, 8, ez)

        def set_stiffness():
            for p in range(5):
                for q in range(5):
                    for r in range(5):
                        w = float(WEIGHTS[p] * WEIGHTS[q] * WEIGHTS[r])
                        for i in range(ex):
                            stiff[p, q, r, i * ey : (i + 1) * ey, :] = modulus_ref[p, i, q, r] * w

        def masks(rec, rows_out, lanes_out, plane_only):
            x = lax.shift_right_logical(rec, shift_x)
            y = lax.shift_right_logical(rec, shift_y) & (ny - 1)
            z = rec & (nz - 1)
            p, i = x & 3, lax.shift_right_logical(x, 2)
            q, j = y & 3, lax.shift_right_logical(y, 2)
            r, l = z & 3, lax.shift_right_logical(z, 2)
            if plane_only:
                row = (q * 4 + r) * 8 + half + j
                row = jnp.where(x == 0, row, -1)
            else:
                row = ((p * 4 + q) * 4 + r) * 8 + i * ey + j
            shape = rows_out.shape
            rows_out[...] = jnp.where(iota(shape, 0) == jnp.broadcast_to(row, shape), 1.0, 0.0)
            shape = lanes_out.shape
            hit = jnp.where(iota(shape, 0) == jnp.broadcast_to(l, shape), 1.0, 0.0)
            lanes_out[...] = hit.astype(BF16)

        def set_scale():
            row8, lane8 = iota((8, ez), 0), iota((8, ez), 1)
            first_x = jnp.logical_and(row8 < ey, me == 0)
            half_x = jnp.where(first_x, 0.5, 1.0).astype(F32)
            half_y = jnp.where((row8 & (ey - 1)) == 0, 0.5, 1.0).astype(F32)
            half_z = jnp.where(lane8 == 0, 0.5, 1.0).astype(F32)
            kept = jnp.where(jnp.logical_and(row8 >= half, has_right), 1.0, 0.0).astype(F32)
            for p in range(5):
                for q in range(4):
                    for r in range(4):
                        weight = float(LINE[p % 4] * LINE[q] * LINE[r])
                        mass = scale[p, q, r] * weight if p < 4 else jnp.where(
                            row8 >= half, scale[p, q, r], 1.0) * weight
                        if p == 0:
                            mass = mass * half_x
                        if q == 0:
                            mass = mass * half_y
                        if r == 0:
                            mass = mass * half_z
                        value = (TIME_STEP * TIME_STEP) / mass
                        scale[p, q, r] = value * kept if p == 4 else value

        def turn(x, by, axis):
            shape = x.shape
            flat_x = x.reshape((-1,) + shape[-2:])
            pieces = [
                pltpu.roll(flat_x[n], by % shape[axis], axis + 2)[None] for n in range(flat_x.shape[0])
            ]
            return jnp.concatenate(pieces, axis=0).reshape(shape)

        def low(shape):
            return iota(shape, len(shape) - 2) < half

        def fill(e):
            shape = (4, 4, 8, ez)
            e[4, 0:4, 0:4] = jnp.where(
                low(shape), turn(e[0, 0:4, 0:4], -ey, -2), e[4, 0:4, 0:4]
            )
            shape = (5, 4, 8, ez)
            inner = (iota(shape, 2) & (ey - 1)) != ey - 1
            e[:, 4, 0:4] = jnp.where(inner, turn(e[:, 0, 0:4], -1, -2), 0.0)
            shape = (5, 5, 8, ez)
            e[:, :, 4] = jnp.where(iota(shape, 3) != ez - 1, turn(e[:, :, 0], -1, -1), 0.0)

        def stencil(e, f, store=None, partner=None, fresh=False):
            @pl.loop(0, 5)
            def _(q):
                g = apply_line(DERIVATIVE, [e[p, q] for p in range(5)])
                for p in range(5):
                    if store is not None:
                        store[0, p, q] = g[p]
                    if partner is not None:
                        product = g[p] * partner[0, p, q]
                        total[p, q] = product if fresh else total[p, q] + product
                if f is not None:
                    back = apply_line(DERIVATIVE.T, [stiff[p, q] * g[p] for p in range(5)])
                    for p in range(5):
                        f[p, q] = back[p]

            @pl.loop(0, 5)
            def _(p):
                g = apply_line(DERIVATIVE, [e[p, q] for q in range(5)])
                for q in range(5):
                    if store is not None:
                        store[1, p, q] = g[q]
                    if partner is not None:
                        total[p, q] = total[p, q] + g[q] * partner[1, p, q]
                if f is not None:
                    back = apply_line(DERIVATIVE.T, [stiff[p, q] * g[q] for q in range(5)])
                    for q in range(5):
                        f[p, q] = f[p, q] + back[q]
                g = apply_line(DERIVATIVE, [e[p, :, r] for r in range(5)])
                for r in range(5):
                    if store is not None:
                        store[2, p, :, r] = g[r]
                    if partner is not None:
                        total[p, :, r] = total[p, :, r] + g[r] * partner[2, p, :, r]
                if f is not None:
                    back = apply_line(DERIVATIVE.T, [stiff[p, :, r] * g[r] for r in range(5)])
                    for r in range(5):
                        f[p, :, r] = f[p, :, r] + back[r]

        def messages(m):
            return (
                to_left(send_l.at[m], recv_r.at[m], ls.at[m], lr.at[m]),
                to_right(send_r.at[m], recv_l.at[m], rs.at[m], rr.at[m]),
            )

        def assemble(f, m):
            shape = (5, 5, 8, ez)
            f[:, :, 0] = f[:, :, 0] + jnp.where(iota(shape, 3) != 0, turn(f[:, :, 4], 1, -1), 0.0)
            shape = (5, 4, 8, ez)
            inner = (iota(shape, 2) & (ey - 1)) != 0
            f[:, 0, 0:4] = f[:, 0, 0:4] + jnp.where(inner, turn(f[:, 4, 0:4], 1, -2), 0.0)
            pair = (2, 4, 8, ez)
            send_l[m] = jnp.where(low(pair), f[0, 0:2, 0:4], turn(f[0, 2:4, 0:4], half, -2))
            send_r[m] = jnp.where(low(pair), turn(f[4, 0:2, 0:4], half, -2), f[4, 2:4, 0:4])
            leftward, rightward = messages(m)

            @pl.when(has_left)
            def _():
                leftward.start()

            @pl.when(has_right)
            def _():
                rightward.start()

            shape = (4, 4, 8, ez)
            f[0, 0:4, 0:4] = f[0, 0:4, 0:4] + jnp.where(
                low(shape), 0.0, turn(f[4, 0:4, 0:4], ey, -2)
            )

        def receive(f, m):
            leftward, rightward = messages(m)

            @pl.when(has_left)
            def _():
                leftward.wait_send()
                rightward.wait_recv()

            @pl.when(has_right)
            def _():
                rightward.wait_send()
                leftward.wait_recv()

            pair = (2, 4, 8, ez)
            near = recv_l[m]
            f[0, 0:2, 0:4] = f[0, 0:2, 0:4] + jnp.where(low(pair), near, 0.0)
            f[0, 2:4, 0:4] = f[0, 2:4, 0:4] + jnp.where(low(pair), turn(near, half, -2), 0.0)
            far = recv_r[m]
            f[4, 0:2, 0:4] = f[4, 0:2, 0:4] + turn(far, half, -2)
            f[4, 2:4, 0:4] = f[4, 2:4, 0:4] + far

        def advance(new, current, old, f, count=5):
            for p in range(count):
                new[p, 0:4, 0:4] = (
                    2.0 * current[p, 0:4, 0:4]
                    - old[p, 0:4, 0:4]
                    - scale[p] * f[p, 0:4, 0:4]
                )

        def read(nodes, rows, lanes):
            x = sum(dot(part, lanes[...]) for part in thirds(nodes))
            return jnp.sum(x * rows[...], axis=0, keepdims=True)

        def spread(source, rows, lanes):
            x = rows[...]
            return sum(
                dot_rows((x * part.astype(F32)).astype(BF16), lanes[...]) for part in thirds(source)
            )

        def records(e):
            return read(e[0:4, 0:4, 0:4].reshape(64 * 8, ez), row_mask, lane_mask)

        def records_h(e):
            return read(e[4, 0:4, 0:4].reshape(16 * 8, ez), row_mask_h, lane_mask_h)

        fu, fl = force.at[0], force.at[1]
        for k in range(4):
            local[k].wait()
        order_own(0)
        local[4].wait()
        order_own(1)
        local[5].wait()
        set_stiffness()
        halo_wait([0])
        order_halo(0)
        fill(u.at[0])
        stencil(u.at[0], fu, store=grads.at[0])
        assemble(fu, 0)
        halo_wait([1])
        order_halo(1)
        fill(lam.at[0])
        stencil(lam.at[0], fl, store=grads.at[last])
        assemble(fl, steps)
        for k in range(6, 12):
            local[k].wait()
        for f in (2, 3, 4):
            order_own(f)
        halo_wait([2, 3, 4])
        for f in (2, 3, 4):
            order_halo(f)
        set_scale()
        share_all(0, sum(obs_ref[n] * obs_ref[n] for n in range(steps)))
        masks(rec_ref[...], row_mask, lane_mask, False)

        def sources_of(e, n):
            residual = records(e) - obs_ref[n - 1]
            residual_h = records_h(e) - halo_obs[n - 1]
            whole = spread(residual / mean_square, row_mask, lane_mask)
            inject[n - 1, 0:4] = whole.reshape(4, 4, 4, 8, ez)
            whole = spread(residual_h / mean_square, row_mask_h, lane_mask_h)
            inject[n - 1, 4] = whole.reshape(4, 4, 8, ez)
            return residual * residual

        residual_sum = jnp.zeros((1, ez), F32)
        receive(fu, 0)
        advance(u.at[1], u.at[0], before.at[0], fu)
        fill(u.at[1])
        for n in range(1, last):
            stencil(u.at[n], fu, store=grads.at[n])
            assemble(fu, n)
            if n == 1:
                halo_wait([5, 6])
                masks(halo_rec[...], row_mask_h, lane_mask_h, True)
                energy = take_all(0)
                mean_square = energy / samples + EPSILON
                receive(fl, steps)
            residual_sum = residual_sum + sources_of(u.at[n], n)
            receive(fu, n)
            advance(u.at[n + 1], u.at[n], u.at[n - 1], fu)
        residual_sum = residual_sum + sources_of(u.at[last], last)
        for k, n in enumerate(range(last, 0, -1)):
            for p in range(5):
                fl[p, 0:4, 0:4] = fl[p, 0:4, 0:4] - inject[n - 1, p]
            advance(lam.at[k + 1], lam.at[k], before.at[1] if k == 0 else lam.at[k - 1], fl)
            fill(lam.at[k + 1])
            if n - 1 > 0:
                stencil(lam.at[k + 1], fl, partner=grads.at[n - 1], fresh=k == 0)
                assemble(fl, steps + 1 + k)
                if k == 0:
                    fill(u.at[last])
                    stencil(u.at[last], fu, partner=grads.at[last])
                    assemble(fu, last)
                receive(fl, steps + 1 + k)
        stencil(lam.at[last], None, partner=grads.at[0])

        flat_total = total.reshape(125 * 8, ez)
        beside = event + 1 - 2 * lax.rem(event, 2)
        across = lax.rem(event + 2, events)
        beyond = lax.rem(beside + 2, events)
        for owner in range(events):
            for i in range(ex):
                pack[owner, i, 120:128] = jnp.zeros((8, ez), F32)
                pack[owner, i, 0:125] = flat_total[pl.ds(i * ey + owner, 125, stride=8), :]

        def reduce_copy(src, slot, there):
            return pltpu.make_async_remote_copy(
                src_ref=src, dst_ref=got.at[slot], send_sem=red_s.at[slot], recv_sem=red_r.at[slot],
                device_id={"event": there}, device_id_type=MESH,
            )

        first = reduce_copy(pack.at[beyond], 0, beside)
        second = reduce_copy(pack.at[beside], 1, beside)
        first.start()
        second.start()
        first.wait()
        relay[...] = pack[across] + got[0]
        third = reduce_copy(relay, 2, across)
        third.start()

        receive(fu, last)
        u3 = u.at[steps]
        advance(u3, u.at[last], u.at[last - 1] if last > 0 else before.at[0], fu, count=4)
        residual = records(u3) - obs_ref[last]
        share_all(1, residual_sum + residual * residual)

        @pl.when(has_left)
        def _():
            for copy in halo_copies:
                copy.wait_send()


        second.wait()
        pair_sum = pack[event] + got[1]
        third.wait()
        cube = jnp.broadcast_to(cube_ref[...][None], (ex, 128, ez))
        value = (pair_sum + got[2]) * cube
        final[...] = value

        top = jnp.max(jnp.abs(value).reshape(ex * 16, 8, ez), axis=0)
        tops_out[0] = top
        tops_in[event] = top
        for k in range(1, events):
            pltpu.make_async_remote_copy(
                src_ref=tops_out.at[0], dst_ref=tops_in.at[event],
                send_sem=top_s.at[k], recv_sem=top_r.at[event],
                device_id={"event": lax.rem(event + k, events)}, device_id_type=MESH,
            ).start()
        for k in range(1, events):
            there = lax.rem(event + k, events)
            copy = pltpu.make_async_remote_copy(
                src_ref=tops_out.at[0], dst_ref=tops_in.at[there],
                send_sem=top_s.at[k], recv_sem=top_r.at[there],
                device_id={"event": there}, device_id_type=MESH,
            )
            copy.wait_send()
            copy.wait_recv()
        top = jnp.max(tops_in[...], axis=0)
        tops_out[1] = top
        tops_far[me] = top

        @pl.loop(1, spaces)
        def _(k):
            pltpu.make_async_remote_copy(
                src_ref=tops_out.at[1], dst_ref=tops_far.at[me],
                send_sem=far_s.at[k], recv_sem=far_r.at[me],
                device_id={"space": lax.rem(me + k, spaces)}, device_id_type=MESH,
            ).start()

        misfit_sum = take_all(1)
        misfit_ref[...] = jnp.broadcast_to(
            0.5 * misfit_sum / (samples * mean_square), misfit_ref.shape
        )

        @pl.loop(1, spaces)
        def _(k):
            there = lax.rem(me + k, spaces)
            copy = pltpu.make_async_remote_copy(
                src_ref=tops_out.at[1], dst_ref=tops_far.at[there],
                send_sem=far_s.at[k], recv_sem=far_r.at[there],
                device_id={"space": there}, device_id_type=MESH,
            )
            copy.wait_send()
            copy.wait_recv()

        top = jnp.max(tops_far[...], axis=0)
        top = jnp.max(jnp.max(top, axis=1, keepdims=True), axis=0, keepdims=True)
        inverse = 1.0 / (top + EPSILON)
        final[...] = final[...] * inverse[None]
        for p in range(5):
            for i in range(ex):
                for q in range(5):
                    at = (p * 5 + q) * 5
                    out_ref[p, i, q, 0] = final[i, at : at + 5, :]

    return kernel


def shards(mesh_shape, now, prev, adj, nxt, modulus, density, receivers, observed):
    events, spaces = mesh_shape["event"], mesh_shape["space"]
    ex, ey, ez = modulus.shape[1], modulus.shape[3], modulus.shape[5]
    steps, count = observed.shape[1], receivers.shape[0]
    assert ex * ey == 8 and ex == 2 and ez == 128 and count == 128 and events == 4 == ey
    assert steps >= 3 and now.shape[0] == 1
    ny, nz = now.shape[2], now.shape[3]
    column, rows, plane, cube = tables(ex, ey, ez)
    kernel = make_kernel(ex, ey, ez, steps, events, spaces, count * spaces)
    vm = lambda *shape: pltpu.VMEM(shape, F32)
    dma = lambda *shape: pltpu.SemaphoreType.DMA(shape)
    rounds = 2 * steps
    scratch = [
        vm(5, 4 * ex, ny, nz), vm(5, ex, 5, 5, ey, ez), pltpu.VMEM((1, count), jnp.int32),
        vm(steps, 1, count), pltpu.VMEM(column.shape, BF16), pltpu.VMEM(rows.shape, BF16),
        pltpu.VMEM(plane.shape, BF16), vm(*cube.shape), dma(12),
        vm(5, ny, nz), pltpu.VMEM((1, count), jnp.int32), vm(steps, 1, count),
        vm(steps + 1, 5, 5, 5, 8, ez), vm(steps, 5, 5, 5, 8, ez), vm(2, 5, 4, 4, 8, ez),
        vm(5, 4, 4, 8, ez), vm(5, 5, 5, 8, ez), vm(steps, 3, 5, 5, 5, 8, ez),
        vm(2, 5, 5, 5, 8, ez), vm(5, 5, 5, 8, ez), vm(steps - 1, 5, 4, 4, 8, ez),
        vm(512, count), pltpu.VMEM((ez, count), BF16), vm(128, count),
        pltpu.VMEM((ez, count), BF16),
        vm(rounds, 2, 4, 8, ez), vm(rounds, 2, 4, 8, ez),
        vm(rounds, 2, 4, 8, ez), vm(rounds, 2, 4, 8, ez),
        vm(2, 8, ez), vm(2, spaces, 8, ez), vm(events, ex, 128, ez), vm(3, ex, 128, ez),
        vm(ex, 128, ez), vm(2, 8, ez), vm(events, 8, ez), vm(spaces, 8, ez), vm(ex, 128, ez),
        dma(7), dma(7), dma(rounds), dma(rounds), dma(rounds), dma(rounds),
        dma(2, spaces), dma(2, spaces), dma(3), dma(3),
        dma(events), dma(events), dma(spaces), dma(spaces),
    ]
    vmem = pl.BlockSpec(memory_space=pltpu.VMEM)
    hbm = pl.BlockSpec(memory_space=pltpu.HBM)
    out, misfit = pl.pallas_call(
        kernel,
        out_shape=(
            jax.ShapeDtypeStruct((5, ex, 5, ey // events, 5, ez), F32),
            jax.ShapeDtypeStruct((1, ez), F32),
        ),
        in_specs=[hbm] * 12,
        out_specs=(vmem, vmem),
        scratch_shapes=scratch,
        compiler_params=pltpu.CompilerParams(
            collective_id=0, has_side_effects=True, vmem_limit_bytes=LIMIT
        ),
        name="window",
    )(
        now, prev, adj, nxt, density, jnp.transpose(modulus, (0, 1, 2, 4, 3, 5)),
        receivers.reshape(1, count), jnp.transpose(observed, (1, 0, 2)),
        jnp.asarray(column), jnp.asarray(rows), jnp.asarray(plane), jnp.asarray(cube),
    )
    return out, misfit[0, :1]


def solution(mesh):
    in_specs = (
        P("event", "space", None, None),
        P("event", "space", None, None),
        P("event", "space", None, None),
        P("event", "space", None, None),
        P(None, "space", None, None, None, None),
        P("space", None, None),
        P("space"),
        P("event", None, "space"),
    )
    out_specs = (P(None, "space", None, "event", None, None), P("event"))
    sizes = dict(mesh.shape)

    def program(*args):
        return shards(sizes, *args)

    return jax.shard_map(program, mesh=mesh, in_specs=in_specs, out_specs=out_specs, check_vma=False)
```

```python
import math

import jax
import jax.numpy as jnp
import numpy as np
from jax import lax
from jax.experimental import pallas as pl
from jax.experimental.pallas import tpu as pltpu
from jax.sharding import PartitionSpec as P

TIME_STEP = 0.05
EPSILON = 1e-06
LIMIT = 64 * 1024 * 1024 - 128 * 1024
F32 = jnp.float32
BF16 = jnp.bfloat16


def gll_tables():
    root = math.sqrt(3.0 / 7.0)
    points = np.array([-1.0, -root, 0.0, root, 1.0])
    weights = np.array([0.1, 49.0 / 90.0, 32.0 / 45.0, 49.0 / 90.0, 0.1])
    legendre = (35.0 * points**4 - 30.0 * points**2 + 3.0) / 8.0
    derivative = np.zeros((5, 5))
    for row in range(5):
        for column in range(5):
            if row != column:
                derivative[row, column] = legendre[row] / (
                    legendre[column] * (points[row] - points[column])
                )
    derivative[0, 0] = -5.0
    derivative[4, 4] = 5.0
    return derivative, weights


DERIVATIVE, WEIGHTS = gll_tables()
LINE = [0.2, 49.0 / 90.0, 32.0 / 45.0, 49.0 / 90.0]


def apply_line(matrix, v):
    m = matrix
    o0, o1 = v[0] - v[4], v[1] - v[3]
    e0, e1 = v[0] + v[4], v[1] + v[3]
    out = [None] * 5
    for s in (0, 1):
        odd = float((m[s, 0] - m[s, 4]) / 2) * o0 + float((m[s, 1] - m[s, 3]) / 2) * o1
        even = (
            float((m[s, 0] + m[s, 4]) / 2) * e0
            + float((m[s, 1] + m[s, 3]) / 2) * e1
            + float(m[s, 2]) * v[2]
        )
        out[s], out[4 - s] = odd + even, odd - even
    out[2] = float(m[2, 0]) * o0 + float(m[2, 1]) * o1
    return out


def thirds(x):
    high = x.astype(BF16)
    rest = x - high.astype(F32)
    mid = rest.astype(BF16)
    return high, mid, (rest - mid.astype(F32)).astype(BF16)


def dot(a, b):
    return jnp.dot(a, b, preferred_element_type=F32)


def dot_rows(a, b):
    return lax.dot_general(a, b, (((1,), (1,)), ((), ())), preferred_element_type=F32)


def make_kernel(ex, ey, ez, steps, events, spaces, receivers_total):
    ny, nz = 4 * ey, 4 * ez
    half = (ex - 1) * ey
    shift_y = int(math.log2(nz))
    shift_x = shift_y + int(math.log2(ny))
    shift_j = int(math.log2(ey))
    last = steps - 1
    samples = steps * receivers_total

    def kernel(
        now_hbm, prev_hbm, adj_hbm, next_hbm, density_hbm, modulus_hbm, rec_hbm, obs_hbm,
        out_ref, misfit_ref,
        fields, modulus_ref, rec_ref, obs_ref, column_ref, sorted_rows, cube_ref, in_sem,
        halo, halo_rec, halo_obs, u, lam, before, scale, stiff, grads, force, total, inject,
        row_mask, lane_mask, row_mask_h, lane_mask_h,
        send_l, send_r, recv_l, recv_r, sums_out, sums_in, pack, got, relay, tops_out, tops_in, tops_far,
        final,
        halo_ss, halo_rs, ls, lr, rs, rr, sum_s, sum_r, red_s, red_r, top_s, top_r, far_s, far_r,
    ):
        me = lax.axis_index("space")
        event = lax.axis_index("event")
        left = jnp.maximum(me - 1, 0)
        right = jnp.minimum(me + 1, spaces - 1)
        has_left, has_right = me > 0, me < spaces - 1
        MESH = pl.DeviceIdType.MESH

        def iota(shape, axis):
            return lax.broadcasted_iota(jnp.int32, shape, axis)

        own = [r.at[0] for r in (now_hbm, adj_hbm, prev_hbm, next_hbm)] + [density_hbm]
        local = [(own[f], fields.at[f]) for f in range(5)]
        local += [(modulus_hbm, modulus_ref), (rec_hbm, rec_ref), (obs_hbm, obs_ref)]
        local = [
            pltpu.make_async_copy(src, dst, in_sem.at[k]) for k, (src, dst) in enumerate(local)
        ]

        barrier = pltpu.get_barrier_semaphore()

        @pl.loop(1, spaces)
        def _(k):
            pl.semaphore_signal(
                barrier, inc=1, device_id={"space": lax.rem(me + k, spaces)}, device_id_type=MESH
            )

        for k in range(1, events):
            pl.semaphore_signal(
                barrier, inc=1, device_id={"event": lax.rem(event + k, events)}, device_id_type=MESH
            )

        for k in (0, 5, 2, 4, 1, 3, 6, 7):
            local[k].start()

        width = 2 * ez
        z, c = iota((width, width), 0), iota((width, width), 1)
        hit = z == 4 * (c & (width // 4 - 1)) + lax.shift_right_logical(c, shift_y - 3)
        column_ref[...] = jnp.where(hit, 1.0, 0.0).astype(BF16)

        def at_point(x):
            edge = jnp.logical_or(x == 0, x == 4)
            w = jnp.where(edge, WEIGHTS[0], jnp.where(x == 2, WEIGHTS[2], WEIGHTS[1]))
            return w.astype(F32)

        point = iota((128, ez), 0)
        p = lax.shift_right_logical(point * 41, 10)
        q = lax.shift_right_logical((point - 25 * p) * 205, 10)
        cube_ref[...] = -at_point(p) * at_point(q) * at_point(point - 25 * p - 5 * q)

        @pl.when(jnp.logical_not(has_right))
        def _():
            halo[0:4] = jnp.zeros((4, ny, nz), F32)
            halo[4] = jnp.ones((ny, nz), F32)
            halo_rec[...] = jnp.zeros_like(halo_rec)
            halo_obs[...] = jnp.zeros_like(halo_obs)
            recv_r[...] = jnp.zeros_like(recv_r)

        @pl.when(jnp.logical_not(has_left))
        def _():
            recv_l[...] = jnp.zeros_like(recv_l)

        pl.semaphore_wait(barrier, spaces - 1 + events - 1)

        def to_left(src, dst, ss, sr):
            return pltpu.make_async_remote_copy(
                src_ref=src, dst_ref=dst, send_sem=ss, recv_sem=sr,
                device_id={"space": left}, device_id_type=MESH,
            )

        def to_right(src, dst, ss, sr):
            return pltpu.make_async_remote_copy(
                src_ref=src, dst_ref=dst, send_sem=ss, recv_sem=sr,
                device_id={"space": right}, device_id_type=MESH,
            )

        halo_copies = [
            to_left(own[f].at[0], halo.at[f], halo_ss.at[f], halo_rs.at[f]) for f in range(5)
        ]
        halo_copies.append(to_left(rec_hbm, halo_rec, halo_ss.at[5], halo_rs.at[5]))
        halo_copies.append(to_left(obs_hbm, halo_obs, halo_ss.at[6], halo_rs.at[6]))

        @pl.when(has_left)
        def _():
            halo_copies[0].start()

        def halo_wait(numbers):
            @pl.when(has_right)
            def _():
                for k in numbers:
                    halo_copies[k].wait_recv()

        def share(slot, k):
            there = lax.rem(me + k, spaces)
            return pltpu.make_async_remote_copy(
                src_ref=sums_out.at[slot], dst_ref=sums_in.at[slot, me],
                send_sem=sum_s.at[slot, k], recv_sem=sum_r.at[slot, me],
                device_id={"space": there}, device_id_type=MESH,
            )

        def taken(slot, k):
            there = lax.rem(me + k, spaces)
            return pltpu.make_async_remote_copy(
                src_ref=sums_out.at[slot], dst_ref=sums_in.at[slot, there],
                send_sem=sum_s.at[slot, k], recv_sem=sum_r.at[slot, there],
                device_id={"space": there}, device_id_type=MESH,
            )

        def share_all(slot, lanes):
            tile = jnp.broadcast_to(lanes, (8, lanes.shape[1]))
            sums_out[slot] = tile
            sums_in[slot, me] = tile

            @pl.loop(1, spaces)
            def _(k):
                share(slot, k).start()

        def take_all(slot):
            @pl.loop(1, spaces)
            def _(k):
                copy = taken(slot, k)
                copy.wait_send()
                copy.wait_recv()

            tile = jnp.sum(sums_in[slot], axis=0)
            return jnp.sum(tile[0:1, :], axis=1, keepdims=True)

        def target(f):
            if f < 2:
                return (u, lam)[f].at[0]
            return before.at[f - 2] if f < 4 else scale

        def sort_columns(nodes):
            count = nodes.shape[0]
            parts = thirds(nodes)
            halves = [part[:, h * width : (h + 1) * width] for h in range(2) for part in parts]
            x = dot(jnp.concatenate(halves, axis=0), column_ref[...])
            x = [x[k * count : (k + 1) * count] for k in range(6)]
            near, far = x[0] + x[1] + x[2], x[3] + x[4] + x[5]
            lower = iota((count, ez), 1) < ez // 2
            for pair in range(2):
                a = near[:, pair * ez : (pair + 1) * ez]
                b = far[:, pair * ez : (pair + 1) * ez]
                sorted_rows[2 * pair, 0:count] = jnp.where(lower, a, pltpu.roll(b, ez // 2, 1))
                sorted_rows[2 * pair + 1, 0:count] = jnp.where(lower, pltpu.roll(a, ez // 2, 1), b)

        def order_own(f):
            local[f].wait()
            sort_columns(fields[f].reshape(4 * ex * ny, nz))
            for r in range(4):
                rows = sorted_rows.at[r]
                for p in range(4):
                    for q in range(4):
                        for i in range(ex):
                            picked = rows[pl.ds((i * 4 + p) * ny + q, ey, stride=4), :]
                            target(f)[p, q, r, i * ey : (i + 1) * ey, :] = picked

        def order_halo(f):
            halo_wait([f])
            sort_columns(halo[f])
            target(f)[4, 0:4, 0:4] = jnp.zeros((4, 4, 8, ez), F32)
            for r in range(4):
                rows = sorted_rows.at[r]
                for q in range(4):
                    target(f)[4, q, r, half : half + ey, :] = rows[pl.ds(q, ey, stride=4), :]

        def set_stiffness():
            for p in range(5):
                for q in range(5):
                    for r in range(5):
                        w = float(WEIGHTS[p] * WEIGHTS[q] * WEIGHTS[r])
                        for i in range(ex):
                            stiff[p, q, r, i * ey : (i + 1) * ey, :] = modulus_ref[p, i, q, r] * w

        def masks(rec, rows_out, lanes_out, plane_only):
            x = lax.shift_right_logical(rec, shift_x)
            y = lax.shift_right_logical(rec, shift_y) & (ny - 1)
            z = rec & (nz - 1)
            p, i = x & 3, lax.shift_right_logical(x, 2)
            q, j = y & 3, lax.shift_right_logical(y, 2)
            r, l = z & 3, lax.shift_right_logical(z, 2)
            if plane_only:
                row = (q * 4 + r) * 8 + half + j
                row = jnp.where(x == 0, row, -1)
            else:
                row = ((p * 4 + q) * 4 + r) * 8 + i * ey + j
            shape = rows_out.shape
            rows_out[...] = jnp.where(iota(shape, 0) == jnp.broadcast_to(row, shape), 1.0, 0.0)
            shape = lanes_out.shape
            hit = jnp.where(iota(shape, 0) == jnp.broadcast_to(l, shape), 1.0, 0.0)
            lanes_out[...] = hit.astype(BF16)

        def set_scale():
            row8, lane8 = iota((8, ez), 0), iota((8, ez), 1)
            first_x = jnp.logical_and(row8 < ey, me == 0)
            half_x = jnp.where(first_x, 0.5, 1.0).astype(F32)
            half_y = jnp.where((row8 & (ey - 1)) == 0, 0.5, 1.0).astype(F32)
            half_z = jnp.where(lane8 == 0, 0.5, 1.0).astype(F32)
            kept = jnp.where(jnp.logical_and(row8 >= half, has_right), 1.0, 0.0).astype(F32)
            for p in range(5):
                for q in range(4):
                    for r in range(4):
                        weight = float(LINE[p % 4] * LINE[q] * LINE[r])
                        mass = scale[p, q, r] * weight if p < 4 else jnp.where(
                            row8 >= half, scale[p, q, r], 1.0) * weight
                        if p == 0:
                            mass = mass * half_x
                        if q == 0:
                            mass = mass * half_y
                        if r == 0:
                            mass = mass * half_z
                        value = (TIME_STEP * TIME_STEP) / mass
                        scale[p, q, r] = value * kept if p == 4 else value

        def turn(x, by, axis):
            shape = x.shape
            flat_x = x.reshape((-1,) + shape[-2:])
            pieces = [
                pltpu.roll(flat_x[n], by % shape[axis], axis + 2)[None] for n in range(flat_x.shape[0])
            ]
            return jnp.concatenate(pieces, axis=0).reshape(shape)

        def low(shape):
            return iota(shape, len(shape) - 2) < half

        def fill(e):
            shape = (4, 4, 8, ez)
            e[4, 0:4, 0:4] = jnp.where(
                low(shape), turn(e[0, 0:4, 0:4], -ey, -2), e[4, 0:4, 0:4]
            )
            shape = (5, 4, 8, ez)
            inner = (iota(shape, 2) & (ey - 1)) != ey - 1
            e[:, 4, 0:4] = jnp.where(inner, turn(e[:, 0, 0:4], -1, -2), 0.0)
            shape = (5, 5, 8, ez)
            e[:, :, 4] = jnp.where(iota(shape, 3) != ez - 1, turn(e[:, :, 0], -1, -1), 0.0)

        def stencil(e, f, store=None, partner=None, fresh=False):
            @pl.loop(0, 5)
            def _(q):
                g = apply_line(DERIVATIVE, [e[p, q] for p in range(5)])
                for p in range(5):
                    if store is not None:
                        store[0, p, q] = g[p]
                    if partner is not None:
                        product = g[p] * partner[0, p, q]
                        total[p, q] = product if fresh else total[p, q] + product
                if f is not None:
                    back = apply_line(DERIVATIVE.T, [stiff[p, q] * g[p] for p in range(5)])
                    for p in range(5):
                        f[p, q] = back[p]

            @pl.loop(0, 5)
            def _(p):
                g = apply_line(DERIVATIVE, [e[p, q] for q in range(5)])
                for q in range(5):
                    if store is not None:
                        store[1, p, q] = g[q]
                    if partner is not None:
                        total[p, q] = total[p, q] + g[q] * partner[1, p, q]
                if f is not None:
                    back = apply_line(DERIVATIVE.T, [stiff[p, q] * g[q] for q in range(5)])
                    for q in range(5):
                        f[p, q] = f[p, q] + back[q]
                g = apply_line(DERIVATIVE, [e[p, :, r] for r in range(5)])
                for r in range(5):
                    if store is not None:
                        store[2, p, :, r] = g[r]
                    if partner is not None:
                        total[p, :, r] = total[p, :, r] + g[r] * partner[2, p, :, r]
                if f is not None:
                    back = apply_line(DERIVATIVE.T, [stiff[p, :, r] * g[r] for r in range(5)])
                    for r in range(5):
                        f[p, :, r] = f[p, :, r] + back[r]

        def messages(m):
            return (
                to_left(send_l.at[m], recv_r.at[m], ls.at[m], lr.at[m]),
                to_right(send_r.at[m], recv_l.at[m], rs.at[m], rr.at[m]),
            )

        def assemble(f, m):
            shape = (5, 5, 8, ez)
            f[:, :, 0] = f[:, :, 0] + jnp.where(iota(shape, 3) != 0, turn(f[:, :, 4], 1, -1), 0.0)
            shape = (5, 4, 8, ez)
            inner = (iota(shape, 2) & (ey - 1)) != 0
            f[:, 0, 0:4] = f[:, 0, 0:4] + jnp.where(inner, turn(f[:, 4, 0:4], 1, -2), 0.0)
            pair = (2, 4, 8, ez)
            send_l[m] = jnp.where(low(pair), f[0, 0:2, 0:4], turn(f[0, 2:4, 0:4], half, -2))
            send_r[m] = jnp.where(low(pair), turn(f[4, 0:2, 0:4], half, -2), f[4, 2:4, 0:4])
            leftward, rightward = messages(m)

            @pl.when(has_left)
            def _():
                leftward.start()

            @pl.when(has_right)
            def _():
                rightward.start()

            shape = (4, 4, 8, ez)
            f[0, 0:4, 0:4] = f[0, 0:4, 0:4] + jnp.where(
                low(shape), 0.0, turn(f[4, 0:4, 0:4], ey, -2)
            )

        def receive(f, m):
            leftward, rightward = messages(m)

            @pl.when(has_left)
            def _():
                leftward.wait_send()
                rightward.wait_recv()

            @pl.when(has_right)
            def _():
                rightward.wait_send()
                leftward.wait_recv()

            pair = (2, 4, 8, ez)
            near = recv_l[m]
            f[0, 0:2, 0:4] = f[0, 0:2, 0:4] + jnp.where(low(pair), near, 0.0)
            f[0, 2:4, 0:4] = f[0, 2:4, 0:4] + jnp.where(low(pair), turn(near, half, -2), 0.0)
            far = recv_r[m]
            f[4, 0:2, 0:4] = f[4, 0:2, 0:4] + turn(far, half, -2)
            f[4, 2:4, 0:4] = f[4, 2:4, 0:4] + far

        def advance(new, current, old, f, count=5):
            for p in range(count):
                new[p, 0:4, 0:4] = (
                    2.0 * current[p, 0:4, 0:4]
                    - old[p, 0:4, 0:4]
                    - scale[p] * f[p, 0:4, 0:4]
                )

        def read(nodes, rows, lanes):
            x = sum(dot(part, lanes[...]) for part in thirds(nodes))
            return jnp.sum(x * rows[...], axis=0, keepdims=True)

        def spread(source, rows, lanes):
            x = rows[...]
            return sum(
                dot_rows((x * part.astype(F32)).astype(BF16), lanes[...]) for part in thirds(source)
            )

        def records(e):
            return read(e[0:4, 0:4, 0:4].reshape(64 * 8, ez), row_mask, lane_mask)

        def records_h(e):
            return read(e[4, 0:4, 0:4].reshape(16 * 8, ez), row_mask_h, lane_mask_h)

        fu, fl = force.at[0], force.at[1]
        order_own(0)

        @pl.when(has_left)
        def _():
            for k in (2, 4, 1, 3, 5, 6):
                halo_copies[k].start()

        local[5].wait()
        set_stiffness()
        order_halo(0)
        fill(u.at[0])
        stencil(u.at[0], fu, store=grads.at[0])
        assemble(fu, 0)
        for f in (2, 4):
            order_own(f)
            order_halo(f)
        set_scale()
        order_own(1)
        order_halo(1)
        fill(lam.at[0])
        local[6].wait()
        local[7].wait()
        share_all(0, sum(obs_ref[n] * obs_ref[n] for n in range(steps)))

        def sources_of(e, n):
            residual = records(e) - obs_ref[n - 1]
            residual_h = records_h(e) - halo_obs[n - 1]
            whole = spread(residual / mean_square, row_mask, lane_mask)
            inject[n - 1, 0:4] = whole.reshape(4, 4, 4, 8, ez)
            whole = spread(residual_h / mean_square, row_mask_h, lane_mask_h)
            inject[n - 1, 4] = whole.reshape(4, 4, 8, ez)
            return residual * residual

        residual_sum = jnp.zeros((1, ez), F32)
        receive(fu, 0)
        advance(u.at[1], u.at[0], before.at[0], fu)
        fill(u.at[1])
        for n in range(1, last):
            stencil(u.at[n], fu, store=grads.at[n])
            assemble(fu, n)
            if n == 1:
                stencil(lam.at[0], fl, store=grads.at[last])
                assemble(fl, steps)
                order_own(3)
                order_halo(3)
                masks(rec_ref[...], row_mask, lane_mask, False)
                halo_wait([5, 6])
                masks(halo_rec[...], row_mask_h, lane_mask_h, True)
                energy = take_all(0)
                mean_square = energy / samples + EPSILON
            residual_sum = residual_sum + sources_of(u.at[n], n)
            receive(fu, n)
            advance(u.at[n + 1], u.at[n], u.at[n - 1], fu)
        residual_sum = residual_sum + sources_of(u.at[last], last)
        receive(fl, steps)

        for k, n in enumerate(range(last, 0, -1)):
            for p in range(5):
                fl[p, 0:4, 0:4] = fl[p, 0:4, 0:4] - inject[n - 1, p]
            advance(lam.at[k + 1], lam.at[k], before.at[1] if k == 0 else lam.at[k - 1], fl)
            fill(lam.at[k + 1])
            if n - 1 > 0:
                stencil(lam.at[k + 1], fl, partner=grads.at[n - 1], fresh=k == 0)
                assemble(fl, steps + 1 + k)
                if k == 0:
                    fill(u.at[last])
                    stencil(u.at[last], fu, partner=grads.at[last])
                    assemble(fu, last)
                receive(fl, steps + 1 + k)
        stencil(lam.at[last], None, partner=grads.at[0])

        flat_total = total.reshape(125 * 8, ez)
        beside = event + 1 - 2 * lax.rem(event, 2)
        across = lax.rem(event + 2, events)
        beyond = lax.rem(beside + 2, events)
        for owner in range(events):
            for i in range(ex):
                pack[owner, i, 120:128] = jnp.zeros((8, ez), F32)
                pack[owner, i, 0:125] = flat_total[pl.ds(i * ey + owner, 125, stride=8), :]

        def reduce_copy(src, slot, there):
            return pltpu.make_async_remote_copy(
                src_ref=src, dst_ref=got.at[slot], send_sem=red_s.at[slot], recv_sem=red_r.at[slot],
                device_id={"event": there}, device_id_type=MESH,
            )

        first = reduce_copy(pack.at[beyond], 0, beside)
        second = reduce_copy(pack.at[beside], 1, beside)
        first.start()
        second.start()
        first.wait()
        relay[...] = pack[across] + got[0]
        third = reduce_copy(relay, 2, across)
        third.start()

        receive(fu, last)
        u3 = u.at[steps]
        advance(u3, u.at[last], u.at[last - 1] if last > 0 else before.at[0], fu, count=4)
        residual = records(u3) - obs_ref[last]
        share_all(1, residual_sum + residual * residual)

        @pl.when(has_left)
        def _():
            for copy in halo_copies:
                copy.wait_send()


        second.wait()
        pair_sum = pack[event] + got[1]
        third.wait()
        value = (pair_sum + got[2]) * cube_ref[...][None]
        final[...] = value

        top = jnp.max(jnp.abs(value).reshape(ex * 16, 8, ez), axis=0)
        tops_out[0] = top
        tops_in[event] = top
        for k in range(1, events):
            pltpu.make_async_remote_copy(
                src_ref=tops_out.at[0], dst_ref=tops_in.at[event],
                send_sem=top_s.at[k], recv_sem=top_r.at[event],
                device_id={"event": lax.rem(event + k, events)}, device_id_type=MESH,
            ).start()
        for k in range(1, events):
            there = lax.rem(event + k, events)
            copy = pltpu.make_async_remote_copy(
                src_ref=tops_out.at[0], dst_ref=tops_in.at[there],
                send_sem=top_s.at[k], recv_sem=top_r.at[there],
                device_id={"event": there}, device_id_type=MESH,
            )
            copy.wait_send()
            copy.wait_recv()
        top = jnp.max(tops_in[...], axis=0)
        tops_out[1] = top
        tops_far[me] = top

        @pl.loop(1, spaces)
        def _(k):
            pltpu.make_async_remote_copy(
                src_ref=tops_out.at[1], dst_ref=tops_far.at[me],
                send_sem=far_s.at[k], recv_sem=far_r.at[me],
                device_id={"space": lax.rem(me + k, spaces)}, device_id_type=MESH,
            ).start()

        misfit_sum = take_all(1)
        misfit_ref[...] = jnp.broadcast_to(
            0.5 * misfit_sum / (samples * mean_square), misfit_ref.shape
        )

        @pl.loop(1, spaces)
        def _(k):
            there = lax.rem(me + k, spaces)
            copy = pltpu.make_async_remote_copy(
                src_ref=tops_out.at[1], dst_ref=tops_far.at[there],
                send_sem=far_s.at[k], recv_sem=far_r.at[there],
                device_id={"space": there}, device_id_type=MESH,
            )
            copy.wait_send()
            copy.wait_recv()

        top = jnp.max(tops_far[...], axis=0)
        top = jnp.max(jnp.max(top, axis=1, keepdims=True), axis=0, keepdims=True)
        inverse = 1.0 / (top + EPSILON)
        final[...] = final[...] * inverse[None]
        for p in range(5):
            for i in range(ex):
                at = (p * ex + i) * 25
                out_ref[at : at + 25, :] = final[i, p * 25 : p * 25 + 25, :]

    return kernel


def shards(mesh_shape, now, prev, adj, nxt, modulus, density, receivers, observed):
    events, spaces = mesh_shape["event"], mesh_shape["space"]
    ex, ey, ez = modulus.shape[1], modulus.shape[3], modulus.shape[5]
    steps, count = observed.shape[1], receivers.shape[0]
    assert ex * ey == 8 and ex == 2 and ez == 128 and count == 128 and events == 4 == ey
    assert steps >= 3 and now.shape[0] == 1
    ny, nz = now.shape[2], now.shape[3]
    kernel = make_kernel(ex, ey, ez, steps, events, spaces, count * spaces)
    vm = lambda *shape: pltpu.VMEM(shape, F32)
    dma = lambda *shape: pltpu.SemaphoreType.DMA(shape)
    rounds = 2 * steps
    scratch = [
        vm(5, 4 * ex, ny, nz), vm(5, ex, 5, 5, ey, ez), pltpu.VMEM((1, count), jnp.int32),
        vm(steps, 1, count), pltpu.VMEM((2 * ez, 2 * ez), BF16), vm(4, 4 * ex * ny, ez),
        vm(128, ez), dma(8),
        vm(5, ny, nz), pltpu.VMEM((1, count), jnp.int32), vm(steps, 1, count),
        vm(steps + 1, 5, 5, 5, 8, ez), vm(steps, 5, 5, 5, 8, ez), vm(2, 5, 4, 4, 8, ez),
        vm(5, 4, 4, 8, ez), vm(5, 5, 5, 8, ez), vm(steps, 3, 5, 5, 5, 8, ez),
        vm(2, 5, 5, 5, 8, ez), vm(5, 5, 5, 8, ez), vm(steps - 1, 5, 4, 4, 8, ez),
        vm(512, count), pltpu.VMEM((ez, count), BF16), vm(128, count),
        pltpu.VMEM((ez, count), BF16),
        vm(rounds, 2, 4, 8, ez), vm(rounds, 2, 4, 8, ez),
        vm(rounds, 2, 4, 8, ez), vm(rounds, 2, 4, 8, ez),
        vm(2, 8, ez), vm(2, spaces, 8, ez), vm(events, ex, 128, ez), vm(3, ex, 128, ez),
        vm(ex, 128, ez), vm(2, 8, ez), vm(events, 8, ez), vm(spaces, 8, ez), vm(ex, 128, ez),
        dma(7), dma(7), dma(rounds), dma(rounds), dma(rounds), dma(rounds),
        dma(2, spaces), dma(2, spaces), dma(3), dma(3),
        dma(events), dma(events), dma(spaces), dma(spaces),
    ]
    vmem = pl.BlockSpec(memory_space=pltpu.VMEM)
    hbm = pl.BlockSpec(memory_space=pltpu.HBM)
    out, misfit = pl.pallas_call(
        kernel,
        out_shape=(
            jax.ShapeDtypeStruct((25 * 5 * ex, ez), F32),
            jax.ShapeDtypeStruct((1, ez), F32),
        ),
        in_specs=[hbm] * 8,
        out_specs=(vmem, vmem),
        scratch_shapes=scratch,
        compiler_params=pltpu.CompilerParams(
            collective_id=0, has_side_effects=True, vmem_limit_bytes=LIMIT
        ),
        name="window",
    )(
        now, prev, adj, nxt, density, jnp.transpose(modulus, (0, 1, 2, 4, 3, 5)),
        receivers.reshape(1, count), jnp.transpose(observed, (1, 0, 2)),
    )
    out = out.reshape(5, ex, 5, 5, 1, ez)
    return jnp.transpose(out, (0, 1, 2, 4, 3, 5)), misfit[0, :1]


def solution(mesh):
    in_specs = (
        P("event", "space", None, None),
        P("event", "space", None, None),
        P("event", "space", None, None),
        P("event", "space", None, None),
        P(None, "space", None, None, None, None),
        P("space", None, None),
        P("space"),
        P("event", None, "space"),
    )
    out_specs = (P(None, "space", None, "event", None, None), P("event"))
    sizes = dict(mesh.shape)

    def program(*args):
        return shards(sizes, *args)

    return jax.shard_map(program, mesh=mesh, in_specs=in_specs, out_specs=out_specs, check_vma=False)
```

```python
import math

import jax
import jax.numpy as jnp
import numpy as np
from jax import lax
from jax.experimental import pallas as pl
from jax.experimental.pallas import tpu as pltpu
from jax.sharding import PartitionSpec as P

TIME_STEP = 0.05
EPSILON = 1e-06
LIMIT = 64 * 1024 * 1024 - 128 * 1024
F32 = jnp.float32
BF16 = jnp.bfloat16


def gll_tables():
    root = math.sqrt(3.0 / 7.0)
    points = np.array([-1.0, -root, 0.0, root, 1.0])
    weights = np.array([0.1, 49.0 / 90.0, 32.0 / 45.0, 49.0 / 90.0, 0.1])
    legendre = (35.0 * points**4 - 30.0 * points**2 + 3.0) / 8.0
    derivative = np.zeros((5, 5))
    for row in range(5):
        for column in range(5):
            if row != column:
                derivative[row, column] = legendre[row] / (
                    legendre[column] * (points[row] - points[column])
                )
    derivative[0, 0] = -5.0
    derivative[4, 4] = 5.0
    return derivative, weights


DERIVATIVE, WEIGHTS = gll_tables()
LINE = [0.2, 49.0 / 90.0, 32.0 / 45.0, 49.0 / 90.0]


def apply_line(matrix, v):
    m = matrix
    o0, o1 = v[0] - v[4], v[1] - v[3]
    e0, e1 = v[0] + v[4], v[1] + v[3]
    out = [None] * 5
    for s in (0, 1):
        odd = float((m[s, 0] - m[s, 4]) / 2) * o0 + float((m[s, 1] - m[s, 3]) / 2) * o1
        even = (
            float((m[s, 0] + m[s, 4]) / 2) * e0
            + float((m[s, 1] + m[s, 3]) / 2) * e1
            + float(m[s, 2]) * v[2]
        )
        out[s], out[4 - s] = odd + even, odd - even
    out[2] = float(m[2, 0]) * o0 + float(m[2, 1]) * o1
    return out


def thirds(x):
    high = x.astype(BF16)
    rest = x - high.astype(F32)
    mid = rest.astype(BF16)
    return high, mid, (rest - mid.astype(F32)).astype(BF16)


def dot(a, b):
    return jnp.dot(a, b, preferred_element_type=F32)


def dot_rows(a, b):
    return lax.dot_general(a, b, (((1,), (1,)), ((), ())), preferred_element_type=F32)


def make_kernel(ex, ey, ez, steps, events, spaces, receivers_total):
    ny, nz = 4 * ey, 4 * ez
    half = (ex - 1) * ey
    shift_y = int(math.log2(nz))
    shift_x = shift_y + int(math.log2(ny))
    shift_j = int(math.log2(ey))
    last = steps - 1
    samples = steps * receivers_total

    def kernel(
        now_hbm, prev_hbm, adj_hbm, next_hbm, density_hbm, modulus_hbm, rec_hbm, obs_hbm,
        out_hbm, side_ref,
        fields, modulus_ref, rec_ref, obs_ref, column_ref, sorted_rows, cube_ref, in_sem,
        halo, halo_rec, halo_obs, u, lam, before, scale, stiff, grads, force, total, inject,
        row_mask, lane_mask, row_mask_h, lane_mask_h,
        send_l, send_r, recv_l, recv_r, sums_out, sums_in, pack, got, relay, tops_out, tops_in, tops_far,
        final,
        out_sem, halo_ss, halo_rs, ls, lr, rs, rr, sum_s, sum_r, red_s, red_r, top_s, top_r, far_s, far_r,
    ):
        me = lax.axis_index("space")
        event = lax.axis_index("event")
        left = jnp.maximum(me - 1, 0)
        right = jnp.minimum(me + 1, spaces - 1)
        has_left, has_right = me > 0, me < spaces - 1
        MESH = pl.DeviceIdType.MESH

        def iota(shape, axis):
            return lax.broadcasted_iota(jnp.int32, shape, axis)

        own = [r.at[0] for r in (now_hbm, adj_hbm, prev_hbm, next_hbm)] + [density_hbm]
        local = [(own[f], fields.at[f]) for f in range(5)]
        local += [(modulus_hbm, modulus_ref), (rec_hbm, rec_ref), (obs_hbm, obs_ref)]
        local = [
            pltpu.make_async_copy(src, dst, in_sem.at[k]) for k, (src, dst) in enumerate(local)
        ]

        barrier = pltpu.get_barrier_semaphore()

        @pl.loop(1, spaces)
        def _(k):
            pl.semaphore_signal(
                barrier, inc=1, device_id={"space": lax.rem(me + k, spaces)}, device_id_type=MESH
            )

        for k in range(1, events):
            pl.semaphore_signal(
                barrier, inc=1, device_id={"event": lax.rem(event + k, events)}, device_id_type=MESH
            )

        for k in (0, 5, 2, 4, 1, 3, 6, 7):
            local[k].start()

        width = 2 * ez
        z, c = iota((width, width), 0), iota((width, width), 1)
        hit = z == 4 * (c & (width // 4 - 1)) + lax.shift_right_logical(c, shift_y - 3)
        column_ref[...] = jnp.where(hit, 1.0, 0.0).astype(BF16)

        def at_point(x):
            edge = jnp.logical_or(x == 0, x == 4)
            w = jnp.where(edge, WEIGHTS[0], jnp.where(x == 2, WEIGHTS[2], WEIGHTS[1]))
            return w.astype(F32)

        point = iota((128, ez), 0)
        p = lax.shift_right_logical(point * 41, 10)
        q = lax.shift_right_logical((point - 25 * p) * 205, 10)
        cube_ref[...] = -at_point(p) * at_point(q) * at_point(point - 25 * p - 5 * q)

        @pl.when(jnp.logical_not(has_right))
        def _():
            halo[0:4] = jnp.zeros((4, ny, nz), F32)
            halo[4] = jnp.ones((ny, nz), F32)
            halo_rec[...] = jnp.zeros_like(halo_rec)
            halo_obs[...] = jnp.zeros_like(halo_obs)
            recv_r[...] = jnp.zeros_like(recv_r)

        @pl.when(jnp.logical_not(has_left))
        def _():
            recv_l[...] = jnp.zeros_like(recv_l)

        pl.semaphore_wait(barrier, spaces - 1 + events - 1)

        def to_left(src, dst, ss, sr):
            return pltpu.make_async_remote_copy(
                src_ref=src, dst_ref=dst, send_sem=ss, recv_sem=sr,
                device_id={"space": left}, device_id_type=MESH,
            )

        def to_right(src, dst, ss, sr):
            return pltpu.make_async_remote_copy(
                src_ref=src, dst_ref=dst, send_sem=ss, recv_sem=sr,
                device_id={"space": right}, device_id_type=MESH,
            )

        halo_copies = [
            to_left(own[f].at[0], halo.at[f], halo_ss.at[f], halo_rs.at[f]) for f in range(5)
        ]
        halo_copies.append(to_left(rec_hbm, halo_rec, halo_ss.at[5], halo_rs.at[5]))
        halo_copies.append(to_left(obs_hbm, halo_obs, halo_ss.at[6], halo_rs.at[6]))

        @pl.when(has_left)
        def _():
            halo_copies[0].start()

        def halo_wait(numbers):
            @pl.when(has_right)
            def _():
                for k in numbers:
                    halo_copies[k].wait_recv()

        def share(slot, k):
            there = lax.rem(me + k, spaces)
            return pltpu.make_async_remote_copy(
                src_ref=sums_out.at[slot], dst_ref=sums_in.at[slot, me],
                send_sem=sum_s.at[slot, k], recv_sem=sum_r.at[slot, me],
                device_id={"space": there}, device_id_type=MESH,
            )

        def taken(slot, k):
            there = lax.rem(me + k, spaces)
            return pltpu.make_async_remote_copy(
                src_ref=sums_out.at[slot], dst_ref=sums_in.at[slot, there],
                send_sem=sum_s.at[slot, k], recv_sem=sum_r.at[slot, there],
                device_id={"space": there}, device_id_type=MESH,
            )

        def share_all(slot, lanes):
            tile = jnp.broadcast_to(lanes, (8, lanes.shape[1]))
            sums_out[slot] = tile
            sums_in[slot, me] = tile

            @pl.loop(1, spaces)
            def _(k):
                share(slot, k).start()

        def take_all(slot):
            @pl.loop(1, spaces)
            def _(k):
                copy = taken(slot, k)
                copy.wait_send()
                copy.wait_recv()

            tile = jnp.sum(sums_in[slot], axis=0)
            return jnp.sum(tile[0:1, :], axis=1, keepdims=True)

        def target(f):
            if f < 2:
                return (u, lam)[f].at[0]
            return before.at[f - 2] if f < 4 else scale

        def sort_columns(nodes):
            count = nodes.shape[0]
            parts = thirds(nodes)
            halves = [part[:, h * width : (h + 1) * width] for h in range(2) for part in parts]
            x = dot(jnp.concatenate(halves, axis=0), column_ref[...])
            x = [x[k * count : (k + 1) * count] for k in range(6)]
            near, far = x[0] + x[1] + x[2], x[3] + x[4] + x[5]
            lower = iota((count, ez), 1) < ez // 2
            for pair in range(2):
                a = near[:, pair * ez : (pair + 1) * ez]
                b = far[:, pair * ez : (pair + 1) * ez]
                sorted_rows[2 * pair, 0:count] = jnp.where(lower, a, pltpu.roll(b, ez // 2, 1))
                sorted_rows[2 * pair + 1, 0:count] = jnp.where(lower, pltpu.roll(a, ez // 2, 1), b)

        def order_own(f):
            local[f].wait()
            sort_columns(fields[f].reshape(4 * ex * ny, nz))
            for r in range(4):
                rows = sorted_rows.at[r]
                for p in range(4):
                    for q in range(4):
                        for i in range(ex):
                            picked = rows[pl.ds((i * 4 + p) * ny + q, ey, stride=4), :]
                            target(f)[p, q, r, i * ey : (i + 1) * ey, :] = picked

        def order_halo(f):
            halo_wait([f])
            sort_columns(halo[f])
            target(f)[4, 0:4, 0:4] = jnp.zeros((4, 4, 8, ez), F32)
            for r in range(4):
                rows = sorted_rows.at[r]
                for q in range(4):
                    target(f)[4, q, r, half : half + ey, :] = rows[pl.ds(q, ey, stride=4), :]

        def set_stiffness():
            for p in range(5):
                for q in range(5):
                    for r in range(5):
                        w = float(WEIGHTS[p] * WEIGHTS[q] * WEIGHTS[r])
                        for i in range(ex):
                            stiff[p, q, r, i * ey : (i + 1) * ey, :] = modulus_ref[p, i, q, r] * w

        def masks(rec, rows_out, lanes_out, plane_only):
            x = lax.shift_right_logical(rec, shift_x)
            y = lax.shift_right_logical(rec, shift_y) & (ny - 1)
            z = rec & (nz - 1)
            p, i = x & 3, lax.shift_right_logical(x, 2)
            q, j = y & 3, lax.shift_right_logical(y, 2)
            r, l = z & 3, lax.shift_right_logical(z, 2)
            if plane_only:
                row = (q * 4 + r) * 8 + half + j
                row = jnp.where(x == 0, row, -1)
            else:
                row = ((p * 4 + q) * 4 + r) * 8 + i * ey + j
            shape = rows_out.shape
            rows_out[...] = jnp.where(iota(shape, 0) == jnp.broadcast_to(row, shape), 1.0, 0.0)
            shape = lanes_out.shape
            hit = jnp.where(iota(shape, 0) == jnp.broadcast_to(l, shape), 1.0, 0.0)
            lanes_out[...] = hit.astype(BF16)

        def set_scale():
            row8, lane8 = iota((8, ez), 0), iota((8, ez), 1)
            first_x = jnp.logical_and(row8 < ey, me == 0)
            half_x = jnp.where(first_x, 0.5, 1.0).astype(F32)
            half_y = jnp.where((row8 & (ey - 1)) == 0, 0.5, 1.0).astype(F32)
            half_z = jnp.where(lane8 == 0, 0.5, 1.0).astype(F32)
            kept = jnp.where(jnp.logical_and(row8 >= half, has_right), 1.0, 0.0).astype(F32)
            for p in range(5):
                for q in range(4):
                    for r in range(4):
                        weight = float(LINE[p % 4] * LINE[q] * LINE[r])
                        mass = scale[p, q, r] * weight if p < 4 else jnp.where(
                            row8 >= half, scale[p, q, r], 1.0) * weight
                        if p == 0:
                            mass = mass * half_x
                        if q == 0:
                            mass = mass * half_y
                        if r == 0:
                            mass = mass * half_z
                        value = (TIME_STEP * TIME_STEP) / mass
                        scale[p, q, r] = value * kept if p == 4 else value

        def turn(x, by, axis):
            shape = x.shape
            flat_x = x.reshape((-1,) + shape[-2:])
            pieces = [
                pltpu.roll(flat_x[n], by % shape[axis], axis + 2)[None] for n in range(flat_x.shape[0])
            ]
            return jnp.concatenate(pieces, axis=0).reshape(shape)

        def low(shape):
            return iota(shape, len(shape) - 2) < half

        def fill(e):
            shape = (4, 4, 8, ez)
            e[4, 0:4, 0:4] = jnp.where(
                low(shape), turn(e[0, 0:4, 0:4], -ey, -2), e[4, 0:4, 0:4]
            )
            shape = (5, 4, 8, ez)
            inner = (iota(shape, 2) & (ey - 1)) != ey - 1
            e[:, 4, 0:4] = jnp.where(inner, turn(e[:, 0, 0:4], -1, -2), 0.0)
            shape = (5, 5, 8, ez)
            e[:, :, 4] = jnp.where(iota(shape, 3) != ez - 1, turn(e[:, :, 0], -1, -1), 0.0)

        def stencil(e, f, store=None, partner=None, fresh=False):
            @pl.loop(0, 5)
            def _(q):
                g = apply_line(DERIVATIVE, [e[p, q] for p in range(5)])
                for p in range(5):
                    if store is not None:
                        store[0, p, q] = g[p]
                    if partner is not None:
                        product = g[p] * partner[0, p, q]
                        total[p, q] = product if fresh else total[p, q] + product
                if f is not None:
                    back = apply_line(DERIVATIVE.T, [stiff[p, q] * g[p] for p in range(5)])
                    for p in range(5):
                        f[p, q] = back[p]

            @pl.loop(0, 5)
            def _(p):
                g = apply_line(DERIVATIVE, [e[p, q] for q in range(5)])
                for q in range(5):
                    if store is not None:
                        store[1, p, q] = g[q]
                    if partner is not None:
                        total[p, q] = total[p, q] + g[q] * partner[1, p, q]
                if f is not None:
                    back = apply_line(DERIVATIVE.T, [stiff[p, q] * g[q] for q in range(5)])
                    for q in range(5):
                        f[p, q] = f[p, q] + back[q]
                g = apply_line(DERIVATIVE, [e[p, :, r] for r in range(5)])
                for r in range(5):
                    if store is not None:
                        store[2, p, :, r] = g[r]
                    if partner is not None:
                        total[p, :, r] = total[p, :, r] + g[r] * partner[2, p, :, r]
                if f is not None:
                    back = apply_line(DERIVATIVE.T, [stiff[p, :, r] * g[r] for r in range(5)])
                    for r in range(5):
                        f[p, :, r] = f[p, :, r] + back[r]

        def messages(m):
            return (
                to_left(send_l.at[m], recv_r.at[m], ls.at[m], lr.at[m]),
                to_right(send_r.at[m], recv_l.at[m], rs.at[m], rr.at[m]),
            )

        def assemble(f, m):
            shape = (5, 5, 8, ez)
            f[:, :, 0] = f[:, :, 0] + jnp.where(iota(shape, 3) != 0, turn(f[:, :, 4], 1, -1), 0.0)
            shape = (5, 4, 8, ez)
            inner = (iota(shape, 2) & (ey - 1)) != 0
            f[:, 0, 0:4] = f[:, 0, 0:4] + jnp.where(inner, turn(f[:, 4, 0:4], 1, -2), 0.0)
            pair = (2, 4, 8, ez)
            send_l[m] = jnp.where(low(pair), f[0, 0:2, 0:4], turn(f[0, 2:4, 0:4], half, -2))
            send_r[m] = jnp.where(low(pair), turn(f[4, 0:2, 0:4], half, -2), f[4, 2:4, 0:4])
            leftward, rightward = messages(m)

            @pl.when(has_left)
            def _():
                leftward.start()

            @pl.when(has_right)
            def _():
                rightward.start()

            shape = (4, 4, 8, ez)
            f[0, 0:4, 0:4] = f[0, 0:4, 0:4] + jnp.where(
                low(shape), 0.0, turn(f[4, 0:4, 0:4], ey, -2)
            )

        def receive(f, m):
            leftward, rightward = messages(m)

            @pl.when(has_left)
            def _():
                leftward.wait_send()
                rightward.wait_recv()

            @pl.when(has_right)
            def _():
                rightward.wait_send()
                leftward.wait_recv()

            pair = (2, 4, 8, ez)
            near = recv_l[m]
            f[0, 0:2, 0:4] = f[0, 0:2, 0:4] + jnp.where(low(pair), near, 0.0)
            f[0, 2:4, 0:4] = f[0, 2:4, 0:4] + jnp.where(low(pair), turn(near, half, -2), 0.0)
            far = recv_r[m]
            f[4, 0:2, 0:4] = f[4, 0:2, 0:4] + turn(far, half, -2)
            f[4, 2:4, 0:4] = f[4, 2:4, 0:4] + far

        def advance(new, current, old, f, count=5):
            for p in range(count):
                new[p, 0:4, 0:4] = (
                    2.0 * current[p, 0:4, 0:4]
                    - old[p, 0:4, 0:4]
                    - scale[p] * f[p, 0:4, 0:4]
                )

        def read(nodes, rows, lanes):
            x = sum(dot(part, lanes[...]) for part in thirds(nodes))
            return jnp.sum(x * rows[...], axis=0, keepdims=True)

        def spread(source, rows, lanes):
            x = rows[...]
            return sum(
                dot_rows((x * part.astype(F32)).astype(BF16), lanes[...]) for part in thirds(source)
            )

        def records(e):
            return read(e[0:4, 0:4, 0:4].reshape(64 * 8, ez), row_mask, lane_mask)

        def records_h(e):
            return read(e[4, 0:4, 0:4].reshape(16 * 8, ez), row_mask_h, lane_mask_h)

        fu, fl = force.at[0], force.at[1]
        order_own(0)

        @pl.when(has_left)
        def _():
            halo_copies[4].start()
            halo_copies[2].start()

        local[5].wait()
        set_stiffness()
        order_halo(0)
        fill(u.at[0])
        stencil(u.at[0], fu, store=grads.at[0])
        assemble(fu, 0)

        @pl.when(has_left)
        def _():
            for k in (1, 5, 6, 3):
                halo_copies[k].start()

        for f in (4, 2):
            order_own(f)
            order_halo(f)
        set_scale()
        order_own(1)
        local[6].wait()
        local[7].wait()
        share_all(0, sum(obs_ref[n] * obs_ref[n] for n in range(steps)))

        def sources_of(e, n):
            residual = records(e) - obs_ref[n - 1]
            residual_h = records_h(e) - halo_obs[n - 1]
            whole = spread(residual / mean_square, row_mask, lane_mask)
            inject[n - 1, 0:4] = whole.reshape(4, 4, 4, 8, ez)
            whole = spread(residual_h / mean_square, row_mask_h, lane_mask_h)
            inject[n - 1, 4] = whole.reshape(4, 4, 8, ez)
            return residual * residual

        residual_sum = jnp.zeros((1, ez), F32)
        receive(fu, 0)
        advance(u.at[1], u.at[0], before.at[0], fu)
        fill(u.at[1])
        for n in range(1, last):
            stencil(u.at[n], fu, store=grads.at[n])
            assemble(fu, n)
            if n == 1:
                order_halo(1)
                fill(lam.at[0])
                stencil(lam.at[0], fl, store=grads.at[last])
                assemble(fl, steps)
                order_own(3)
                order_halo(3)
                masks(rec_ref[...], row_mask, lane_mask, False)
                halo_wait([5, 6])
                masks(halo_rec[...], row_mask_h, lane_mask_h, True)
                energy = take_all(0)
                mean_square = energy / samples + EPSILON
            residual_sum = residual_sum + sources_of(u.at[n], n)
            receive(fu, n)
            advance(u.at[n + 1], u.at[n], u.at[n - 1], fu)
        residual_sum = residual_sum + sources_of(u.at[last], last)
        receive(fl, steps)

        for k, n in enumerate(range(last, 0, -1)):
            for p in range(5):
                fl[p, 0:4, 0:4] = fl[p, 0:4, 0:4] - inject[n - 1, p]
            advance(lam.at[k + 1], lam.at[k], before.at[1] if k == 0 else lam.at[k - 1], fl)
            fill(lam.at[k + 1])
            if n - 1 > 0:
                stencil(lam.at[k + 1], fl, partner=grads.at[n - 1], fresh=k == 0)
                assemble(fl, steps + 1 + k)
                if k == 0:
                    fill(u.at[last])
                    stencil(u.at[last], fu, partner=grads.at[last])
                    assemble(fu, last)
                receive(fl, steps + 1 + k)
        stencil(lam.at[last], None, partner=grads.at[0])

        flat_total = total.reshape(125 * 8, ez)
        beside = event + 1 - 2 * lax.rem(event, 2)
        across = lax.rem(event + 2, events)
        beyond = lax.rem(beside + 2, events)
        for owner in range(events):
            for i in range(ex):
                pack[owner, i, 120:128] = jnp.zeros((8, ez), F32)
                pack[owner, i, 0:125] = flat_total[pl.ds(i * ey + owner, 125, stride=8), :]

        def reduce_copy(src, slot, there):
            return pltpu.make_async_remote_copy(
                src_ref=src, dst_ref=got.at[slot], send_sem=red_s.at[slot], recv_sem=red_r.at[slot],
                device_id={"event": there}, device_id_type=MESH,
            )

        first = reduce_copy(pack.at[beyond], 0, beside)
        second = reduce_copy(pack.at[beside], 1, beside)
        first.start()
        second.start()
        first.wait()
        relay[...] = pack[across] + got[0]
        third = reduce_copy(relay, 2, across)
        third.start()

        receive(fu, last)
        u3 = u.at[steps]
        advance(u3, u.at[last], u.at[last - 1] if last > 0 else before.at[0], fu, count=4)
        residual = records(u3) - obs_ref[last]
        share_all(1, residual_sum + residual * residual)

        @pl.when(has_left)
        def _():
            for copy in halo_copies:
                copy.wait_send()


        second.wait()
        pair_sum = pack[event] + got[1]
        third.wait()
        value = (pair_sum + got[2]) * cube_ref[...][None]
        for p in range(5):
            for i in range(ex):
                at = (p * ex + i) * 25
                final[at : at + 25, 0, :] = value[i, p * 25 : p * 25 + 25, :]
        out_copy = pltpu.make_async_copy(final, out_hbm, out_sem)
        out_copy.start()

        top = jnp.max(jnp.abs(value).reshape(ex * 16, 8, ez), axis=0)
        tops_out[0] = top
        tops_in[event] = top
        for k in range(1, events):
            pltpu.make_async_remote_copy(
                src_ref=tops_out.at[0], dst_ref=tops_in.at[event],
                send_sem=top_s.at[k], recv_sem=top_r.at[event],
                device_id={"event": lax.rem(event + k, events)}, device_id_type=MESH,
            ).start()
        for k in range(1, events):
            there = lax.rem(event + k, events)
            copy = pltpu.make_async_remote_copy(
                src_ref=tops_out.at[0], dst_ref=tops_in.at[there],
                send_sem=top_s.at[k], recv_sem=top_r.at[there],
                device_id={"event": there}, device_id_type=MESH,
            )
            copy.wait_send()
            copy.wait_recv()
        top = jnp.max(tops_in[...], axis=0)
        tops_out[1] = top
        tops_far[me] = top

        @pl.loop(1, spaces)
        def _(k):
            pltpu.make_async_remote_copy(
                src_ref=tops_out.at[1], dst_ref=tops_far.at[me],
                send_sem=far_s.at[k], recv_sem=far_r.at[me],
                device_id={"space": lax.rem(me + k, spaces)}, device_id_type=MESH,
            ).start()

        misfit_sum = take_all(1)
        misfit = 0.5 * misfit_sum / (samples * mean_square)
        side_ref[0:1] = jnp.broadcast_to(misfit, (1, ez))

        @pl.loop(1, spaces)
        def _(k):
            there = lax.rem(me + k, spaces)
            copy = pltpu.make_async_remote_copy(
                src_ref=tops_out.at[1], dst_ref=tops_far.at[there],
                send_sem=far_s.at[k], recv_sem=far_r.at[there],
                device_id={"space": there}, device_id_type=MESH,
            )
            copy.wait_send()
            copy.wait_recv()

        top = jnp.max(tops_far[...], axis=0)
        top = jnp.max(jnp.max(top, axis=1, keepdims=True), axis=0, keepdims=True)
        side_ref[1:2] = jnp.broadcast_to(1.0 / (top + EPSILON), (1, ez))
        out_copy.wait()

    return kernel


def shards(mesh_shape, now, prev, adj, nxt, modulus, density, receivers, observed):
    events, spaces = mesh_shape["event"], mesh_shape["space"]
    ex, ey, ez = modulus.shape[1], modulus.shape[3], modulus.shape[5]
    steps, count = observed.shape[1], receivers.shape[0]
    assert ex * ey == 8 and ex == 2 and ez == 128 and count == 128 and events == 4 == ey
    assert steps >= 3 and now.shape[0] == 1
    ny, nz = now.shape[2], now.shape[3]
    kernel = make_kernel(ex, ey, ez, steps, events, spaces, count * spaces)
    vm = lambda *shape: pltpu.VMEM(shape, F32)
    dma = lambda *shape: pltpu.SemaphoreType.DMA(shape)
    rounds = 2 * steps
    scratch = [
        vm(5, 4 * ex, ny, nz), vm(5, ex, 5, 5, ey, ez), pltpu.VMEM((1, count), jnp.int32),
        vm(steps, 1, count), pltpu.VMEM((2 * ez, 2 * ez), BF16), vm(4, 4 * ex * ny, ez),
        vm(128, ez), dma(8),
        vm(5, ny, nz), pltpu.VMEM((1, count), jnp.int32), vm(steps, 1, count),
        vm(steps + 1, 5, 5, 5, 8, ez), vm(steps, 5, 5, 5, 8, ez), vm(2, 5, 4, 4, 8, ez),
        vm(5, 4, 4, 8, ez), vm(5, 5, 5, 8, ez), vm(steps, 3, 5, 5, 5, 8, ez),
        vm(2, 5, 5, 5, 8, ez), vm(5, 5, 5, 8, ez), vm(steps - 1, 5, 4, 4, 8, ez),
        vm(512, count), pltpu.VMEM((ez, count), BF16), vm(128, count),
        pltpu.VMEM((ez, count), BF16),
        vm(rounds, 2, 4, 8, ez), vm(rounds, 2, 4, 8, ez),
        vm(rounds, 2, 4, 8, ez), vm(rounds, 2, 4, 8, ez),
        vm(2, 8, ez), vm(2, spaces, 8, ez), vm(events, ex, 128, ez), vm(3, ex, 128, ez),
        vm(ex, 128, ez), vm(2, 8, ez), vm(events, 8, ez), vm(spaces, 8, ez), vm(25 * 5 * ex, 1, ez),
        pltpu.SemaphoreType.DMA,
        dma(7), dma(7), dma(rounds), dma(rounds), dma(rounds), dma(rounds),
        dma(2, spaces), dma(2, spaces), dma(3), dma(3),
        dma(events), dma(events), dma(spaces), dma(spaces),
    ]
    vmem = pl.BlockSpec(memory_space=pltpu.VMEM)
    hbm = pl.BlockSpec(memory_space=pltpu.HBM)
    out, side = pl.pallas_call(
        kernel,
        out_shape=(
            jax.ShapeDtypeStruct((25 * 5 * ex, 1, ez), F32),
            jax.ShapeDtypeStruct((2, ez), F32),
        ),
        in_specs=[hbm] * 8,
        out_specs=(hbm, vmem),
        scratch_shapes=scratch,
        compiler_params=pltpu.CompilerParams(
            collective_id=0, has_side_effects=True, vmem_limit_bytes=LIMIT
        ),
        name="window",
    )(
        now, prev, adj, nxt, density, jnp.transpose(modulus, (0, 1, 2, 4, 3, 5)),
        receivers.reshape(1, count), jnp.transpose(observed, (1, 0, 2)),
    )
    out = jnp.transpose(out.reshape(5, ex, 5, 5, 1, ez), (0, 1, 2, 4, 3, 5))
    return out * side[1, 0], side[0, :1]


def solution(mesh):
    in_specs = (
        P("event", "space", None, None),
        P("event", "space", None, None),
        P("event", "space", None, None),
        P("event", "space", None, None),
        P(None, "space", None, None, None, None),
        P("space", None, None),
        P("space"),
        P("event", None, "space"),
    )
    out_specs = (P(None, "space", None, "event", None, None), P("event"))
    sizes = dict(mesh.shape)

    def program(*args):
        return shards(sizes, *args)

    return jax.shard_map(program, mesh=mesh, in_specs=in_specs, out_specs=out_specs, check_vma=False)
```

```python
import math

import jax
import jax.numpy as jnp
import numpy as np
from jax import lax
from jax.experimental import pallas as pl
from jax.experimental.pallas import tpu as pltpu
from jax.sharding import PartitionSpec as P

TIME_STEP = 0.05
EPSILON = 1e-06
LIMIT = 64 * 1024 * 1024 - 128 * 1024
F32 = jnp.float32
BF16 = jnp.bfloat16


def gll_tables():
    root = math.sqrt(3.0 / 7.0)
    points = np.array([-1.0, -root, 0.0, root, 1.0])
    weights = np.array([0.1, 49.0 / 90.0, 32.0 / 45.0, 49.0 / 90.0, 0.1])
    legendre = (35.0 * points**4 - 30.0 * points**2 + 3.0) / 8.0
    derivative = np.zeros((5, 5))
    for row in range(5):
        for column in range(5):
            if row != column:
                derivative[row, column] = legendre[row] / (
                    legendre[column] * (points[row] - points[column])
                )
    derivative[0, 0] = -5.0
    derivative[4, 4] = 5.0
    return derivative, weights


DERIVATIVE, WEIGHTS = gll_tables()
LINE = [0.2, 49.0 / 90.0, 32.0 / 45.0, 49.0 / 90.0]


def apply_line(matrix, v):
    m = matrix
    o0, o1 = v[0] - v[4], v[1] - v[3]
    e0, e1 = v[0] + v[4], v[1] + v[3]
    out = [None] * 5
    for s in (0, 1):
        odd = float((m[s, 0] - m[s, 4]) / 2) * o0 + float((m[s, 1] - m[s, 3]) / 2) * o1
        even = (
            float((m[s, 0] + m[s, 4]) / 2) * e0
            + float((m[s, 1] + m[s, 3]) / 2) * e1
            + float(m[s, 2]) * v[2]
        )
        out[s], out[4 - s] = odd + even, odd - even
    out[2] = float(m[2, 0]) * o0 + float(m[2, 1]) * o1
    return out


def thirds(x):
    high = x.astype(BF16)
    rest = x - high.astype(F32)
    mid = rest.astype(BF16)
    return high, mid, (rest - mid.astype(F32)).astype(BF16)


def dot(a, b):
    return jnp.dot(a, b, preferred_element_type=F32)


def dot_rows(a, b):
    return lax.dot_general(a, b, (((1,), (1,)), ((), ())), preferred_element_type=F32)


def make_kernel(ex, ey, ez, steps, events, spaces, receivers_total):
    ny, nz = 4 * ey, 4 * ez
    half = (ex - 1) * ey
    shift_y = int(math.log2(nz))
    shift_x = shift_y + int(math.log2(ny))
    shift_j = int(math.log2(ey))
    last = steps - 1
    samples = steps * receivers_total

    def kernel(
        now_hbm, prev_hbm, adj_hbm, next_hbm, density_hbm, modulus_hbm, rec_hbm, obs_hbm,
        out_ref, side_ref,
        fields, modulus_ref, rec_ref, obs_ref, column_ref, sorted_rows, cube_ref, in_sem,
        halo, halo_rec, halo_obs, u, lam, before, scale, stiff, grads, force, total, inject,
        row_mask, lane_mask, row_mask_h, lane_mask_h,
        send_l, send_r, recv_l, recv_r, sums_out, sums_in, pack, got, relay, tops_out, tops_in, tops_far,
        final,
        halo_ss, halo_rs, ls, lr, rs, rr, sum_s, sum_r, red_s, red_r, top_s, top_r, far_s, far_r,
    ):
        me = lax.axis_index("space")
        event = lax.axis_index("event")
        left = jnp.maximum(me - 1, 0)
        right = jnp.minimum(me + 1, spaces - 1)
        has_left, has_right = me > 0, me < spaces - 1
        MESH = pl.DeviceIdType.MESH

        def iota(shape, axis):
            return lax.broadcasted_iota(jnp.int32, shape, axis)

        own = [r.at[0] for r in (now_hbm, adj_hbm, prev_hbm, next_hbm)] + [density_hbm]
        local = [(own[f], fields.at[f]) for f in range(5)]
        local += [(modulus_hbm, modulus_ref), (rec_hbm, rec_ref), (obs_hbm, obs_ref)]
        local = [
            pltpu.make_async_copy(src, dst, in_sem.at[k]) for k, (src, dst) in enumerate(local)
        ]

        barrier = pltpu.get_barrier_semaphore()

        @pl.loop(1, spaces)
        def _(k):
            pl.semaphore_signal(
                barrier, inc=1, device_id={"space": lax.rem(me + k, spaces)}, device_id_type=MESH
            )

        for k in range(1, events):
            pl.semaphore_signal(
                barrier, inc=1, device_id={"event": lax.rem(event + k, events)}, device_id_type=MESH
            )

        for k in (0, 5, 2, 4, 1, 3, 6, 7):
            local[k].start()

        width = 2 * ez
        z, c = iota((width, width), 0), iota((width, width), 1)
        hit = z == 4 * (c & (width // 4 - 1)) + lax.shift_right_logical(c, shift_y - 3)
        column_ref[...] = jnp.where(hit, 1.0, 0.0).astype(BF16)

        def at_point(x):
            edge = jnp.logical_or(x == 0, x == 4)
            w = jnp.where(edge, WEIGHTS[0], jnp.where(x == 2, WEIGHTS[2], WEIGHTS[1]))
            return w.astype(F32)

        point = iota((128, ez), 0)
        p = lax.shift_right_logical(point * 41, 10)
        q = lax.shift_right_logical((point - 25 * p) * 205, 10)
        cube_ref[...] = -at_point(p) * at_point(q) * at_point(point - 25 * p - 5 * q)

        @pl.when(jnp.logical_not(has_right))
        def _():
            halo[0:4] = jnp.zeros((4, ny, nz), F32)
            halo[4] = jnp.ones((ny, nz), F32)
            halo_rec[...] = jnp.zeros_like(halo_rec)
            halo_obs[...] = jnp.zeros_like(halo_obs)
            recv_r[...] = jnp.zeros_like(recv_r)

        @pl.when(jnp.logical_not(has_left))
        def _():
            recv_l[...] = jnp.zeros_like(recv_l)

        pl.semaphore_wait(barrier, spaces - 1 + events - 1)

        def to_left(src, dst, ss, sr):
            return pltpu.make_async_remote_copy(
                src_ref=src, dst_ref=dst, send_sem=ss, recv_sem=sr,
                device_id={"space": left}, device_id_type=MESH,
            )

        def to_right(src, dst, ss, sr):
            return pltpu.make_async_remote_copy(
                src_ref=src, dst_ref=dst, send_sem=ss, recv_sem=sr,
                device_id={"space": right}, device_id_type=MESH,
            )

        halo_copies = [
            to_left(own[f].at[0], halo.at[f], halo_ss.at[f], halo_rs.at[f]) for f in range(5)
        ]
        halo_copies.append(to_left(rec_hbm, halo_rec, halo_ss.at[5], halo_rs.at[5]))
        halo_copies.append(to_left(obs_hbm, halo_obs, halo_ss.at[6], halo_rs.at[6]))

        @pl.when(has_left)
        def _():
            halo_copies[0].start()

        def halo_wait(numbers):
            @pl.when(has_right)
            def _():
                for k in numbers:
                    halo_copies[k].wait_recv()

        def share(slot, k):
            there = lax.rem(me + k, spaces)
            return pltpu.make_async_remote_copy(
                src_ref=sums_out.at[slot], dst_ref=sums_in.at[slot, me],
                send_sem=sum_s.at[slot, k], recv_sem=sum_r.at[slot, me],
                device_id={"space": there}, device_id_type=MESH,
            )

        def taken(slot, k):
            there = lax.rem(me + k, spaces)
            return pltpu.make_async_remote_copy(
                src_ref=sums_out.at[slot], dst_ref=sums_in.at[slot, there],
                send_sem=sum_s.at[slot, k], recv_sem=sum_r.at[slot, there],
                device_id={"space": there}, device_id_type=MESH,
            )

        def share_all(slot, lanes):
            tile = jnp.broadcast_to(lanes, (8, lanes.shape[1]))
            sums_out[slot] = tile
            sums_in[slot, me] = tile

            @pl.loop(1, spaces)
            def _(k):
                share(slot, k).start()

        def take_all(slot):
            @pl.loop(1, spaces)
            def _(k):
                copy = taken(slot, k)
                copy.wait_send()
                copy.wait_recv()

            tile = jnp.sum(sums_in[slot], axis=0)
            return jnp.sum(tile[0:1, :], axis=1, keepdims=True)

        def target(f):
            if f < 2:
                return (u, lam)[f].at[0]
            return before.at[f - 2] if f < 4 else scale

        def sort_columns(nodes):
            count = nodes.shape[0]
            parts = thirds(nodes)
            halves = [part[:, h * width : (h + 1) * width] for h in range(2) for part in parts]
            x = dot(jnp.concatenate(halves, axis=0), column_ref[...])
            x = [x[k * count : (k + 1) * count] for k in range(6)]
            near, far = x[0] + x[1] + x[2], x[3] + x[4] + x[5]
            lower = iota((count, ez), 1) < ez // 2
            for pair in range(2):
                a = near[:, pair * ez : (pair + 1) * ez]
                b = far[:, pair * ez : (pair + 1) * ez]
                sorted_rows[2 * pair, 0:count] = jnp.where(lower, a, pltpu.roll(b, ez // 2, 1))
                sorted_rows[2 * pair + 1, 0:count] = jnp.where(lower, pltpu.roll(a, ez // 2, 1), b)

        def order_own(f):
            local[f].wait()
            sort_columns(fields[f].reshape(4 * ex * ny, nz))
            for r in range(4):
                rows = sorted_rows.at[r]
                for p in range(4):
                    for q in range(4):
                        for i in range(ex):
                            picked = rows[pl.ds((i * 4 + p) * ny + q, ey, stride=4), :]
                            target(f)[p, q, r, i * ey : (i + 1) * ey, :] = picked

        def order_halo(f):
            halo_wait([f])
            sort_columns(halo[f])
            target(f)[4, 0:4, 0:4] = jnp.zeros((4, 4, 8, ez), F32)
            for r in range(4):
                rows = sorted_rows.at[r]
                for q in range(4):
                    target(f)[4, q, r, half : half + ey, :] = rows[pl.ds(q, ey, stride=4), :]

        def set_stiffness():
            for p in range(5):
                for q in range(5):
                    for r in range(5):
                        w = float(WEIGHTS[p] * WEIGHTS[q] * WEIGHTS[r])
                        for i in range(ex):
                            stiff[p, q, r, i * ey : (i + 1) * ey, :] = modulus_ref[p, i, q, r] * w

        def masks(rec, rows_out, lanes_out, plane_only):
            x = lax.shift_right_logical(rec, shift_x)
            y = lax.shift_right_logical(rec, shift_y) & (ny - 1)
            z = rec & (nz - 1)
            p, i = x & 3, lax.shift_right_logical(x, 2)
            q, j = y & 3, lax.shift_right_logical(y, 2)
            r, l = z & 3, lax.shift_right_logical(z, 2)
            if plane_only:
                row = (q * 4 + r) * 8 + half + j
                row = jnp.where(x == 0, row, -1)
            else:
                row = ((p * 4 + q) * 4 + r) * 8 + i * ey + j
            shape = rows_out.shape
            rows_out[...] = jnp.where(iota(shape, 0) == jnp.broadcast_to(row, shape), 1.0, 0.0)
            shape = lanes_out.shape
            hit = jnp.where(iota(shape, 0) == jnp.broadcast_to(l, shape), 1.0, 0.0)
            lanes_out[...] = hit.astype(BF16)

        def set_scale():
            row8, lane8 = iota((8, ez), 0), iota((8, ez), 1)
            first_x = jnp.logical_and(row8 < ey, me == 0)
            half_x = jnp.where(first_x, 0.5, 1.0).astype(F32)
            half_y = jnp.where((row8 & (ey - 1)) == 0, 0.5, 1.0).astype(F32)
            half_z = jnp.where(lane8 == 0, 0.5, 1.0).astype(F32)
            kept = jnp.where(jnp.logical_and(row8 >= half, has_right), 1.0, 0.0).astype(F32)
            for p in range(5):
                for q in range(4):
                    for r in range(4):
                        weight = float(LINE[p % 4] * LINE[q] * LINE[r])
                        mass = scale[p, q, r] * weight if p < 4 else jnp.where(
                            row8 >= half, scale[p, q, r], 1.0) * weight
                        if p == 0:
                            mass = mass * half_x
                        if q == 0:
                            mass = mass * half_y
                        if r == 0:
                            mass = mass * half_z
                        value = (TIME_STEP * TIME_STEP) / mass
                        scale[p, q, r] = value * kept if p == 4 else value

        def turn(x, by, axis):
            shape = x.shape
            flat_x = x.reshape((-1,) + shape[-2:])
            pieces = [
                pltpu.roll(flat_x[n], by % shape[axis], axis + 2)[None] for n in range(flat_x.shape[0])
            ]
            return jnp.concatenate(pieces, axis=0).reshape(shape)

        def low(shape):
            return iota(shape, len(shape) - 2) < half

        def fill(e):
            shape = (4, 4, 8, ez)
            e[4, 0:4, 0:4] = jnp.where(
                low(shape), turn(e[0, 0:4, 0:4], -ey, -2), e[4, 0:4, 0:4]
            )
            shape = (5, 4, 8, ez)
            inner = (iota(shape, 2) & (ey - 1)) != ey - 1
            e[:, 4, 0:4] = jnp.where(inner, turn(e[:, 0, 0:4], -1, -2), 0.0)
            shape = (5, 5, 8, ez)
            e[:, :, 4] = jnp.where(iota(shape, 3) != ez - 1, turn(e[:, :, 0], -1, -1), 0.0)

        def stencil(e, f, store=None, partner=None, fresh=False):
            @pl.loop(0, 5, unroll=True)
            def _(q):
                g = apply_line(DERIVATIVE, [e[p, q] for p in range(5)])
                for p in range(5):
                    if store is not None:
                        store[0, p, q] = g[p]
                    if partner is not None:
                        product = g[p] * partner[0, p, q]
                        total[p, q] = product if fresh else total[p, q] + product
                if f is not None:
                    back = apply_line(DERIVATIVE.T, [stiff[p, q] * g[p] for p in range(5)])
                    for p in range(5):
                        f[p, q] = back[p]

            @pl.loop(0, 5, unroll=True)
            def _(p):
                g = apply_line(DERIVATIVE, [e[p, q] for q in range(5)])
                for q in range(5):
                    if store is not None:
                        store[1, p, q] = g[q]
                    if partner is not None:
                        total[p, q] = total[p, q] + g[q] * partner[1, p, q]
                if f is not None:
                    back = apply_line(DERIVATIVE.T, [stiff[p, q] * g[q] for q in range(5)])
                    for q in range(5):
                        f[p, q] = f[p, q] + back[q]
                g = apply_line(DERIVATIVE, [e[p, :, r] for r in range(5)])
                for r in range(5):
                    if store is not None:
                        store[2, p, :, r] = g[r]
                    if partner is not None:
                        total[p, :, r] = total[p, :, r] + g[r] * partner[2, p, :, r]
                if f is not None:
                    back = apply_line(DERIVATIVE.T, [stiff[p, :, r] * g[r] for r in range(5)])
                    for r in range(5):
                        f[p, :, r] = f[p, :, r] + back[r]

        def messages(m):
            return (
                to_left(send_l.at[m], recv_r.at[m], ls.at[m], lr.at[m]),
                to_right(send_r.at[m], recv_l.at[m], rs.at[m], rr.at[m]),
            )

        def assemble(f, m):
            shape = (5, 5, 8, ez)
            f[:, :, 0] = f[:, :, 0] + jnp.where(iota(shape, 3) != 0, turn(f[:, :, 4], 1, -1), 0.0)
            shape = (5, 4, 8, ez)
            inner = (iota(shape, 2) & (ey - 1)) != 0
            f[:, 0, 0:4] = f[:, 0, 0:4] + jnp.where(inner, turn(f[:, 4, 0:4], 1, -2), 0.0)
            pair = (2, 4, 8, ez)
            send_l[m] = jnp.where(low(pair), f[0, 0:2, 0:4], turn(f[0, 2:4, 0:4], half, -2))
            send_r[m] = jnp.where(low(pair), turn(f[4, 0:2, 0:4], half, -2), f[4, 2:4, 0:4])
            leftward, rightward = messages(m)

            @pl.when(has_left)
            def _():
                leftward.start()

            @pl.when(has_right)
            def _():
                rightward.start()

            shape = (4, 4, 8, ez)
            f[0, 0:4, 0:4] = f[0, 0:4, 0:4] + jnp.where(
                low(shape), 0.0, turn(f[4, 0:4, 0:4], ey, -2)
            )

        def receive(f, m):
            leftward, rightward = messages(m)

            @pl.when(has_left)
            def _():
                leftward.wait_send()
                rightward.wait_recv()

            @pl.when(has_right)
            def _():
                rightward.wait_send()
                leftward.wait_recv()

            pair = (2, 4, 8, ez)
            near = recv_l[m]
            f[0, 0:2, 0:4] = f[0, 0:2, 0:4] + jnp.where(low(pair), near, 0.0)
            f[0, 2:4, 0:4] = f[0, 2:4, 0:4] + jnp.where(low(pair), turn(near, half, -2), 0.0)
            far = recv_r[m]
            f[4, 0:2, 0:4] = f[4, 0:2, 0:4] + turn(far, half, -2)
            f[4, 2:4, 0:4] = f[4, 2:4, 0:4] + far

        def advance(new, current, old, f, count=5):
            for p in range(count):
                new[p, 0:4, 0:4] = (
                    2.0 * current[p, 0:4, 0:4]
                    - old[p, 0:4, 0:4]
                    - scale[p] * f[p, 0:4, 0:4]
                )

        def read(nodes, rows, lanes):
            x = sum(dot(part, lanes[...]) for part in thirds(nodes))
            return jnp.sum(x * rows[...], axis=0, keepdims=True)

        def spread(source, rows, lanes):
            x = rows[...]
            return sum(
                dot_rows((x * part.astype(F32)).astype(BF16), lanes[...]) for part in thirds(source)
            )

        def records(e):
            return read(e[0:4, 0:4, 0:4].reshape(64 * 8, ez), row_mask, lane_mask)

        def records_h(e):
            return read(e[4, 0:4, 0:4].reshape(16 * 8, ez), row_mask_h, lane_mask_h)

        fu, fl = force.at[0], force.at[1]
        order_own(0)

        @pl.when(has_left)
        def _():
            halo_copies[4].start()
            halo_copies[2].start()

        local[5].wait()
        set_stiffness()
        order_halo(0)
        fill(u.at[0])
        stencil(u.at[0], fu, store=grads.at[0])
        assemble(fu, 0)

        @pl.when(has_left)
        def _():
            for k in (1, 5, 6, 3):
                halo_copies[k].start()

        for f in (4, 2):
            order_own(f)
            order_halo(f)
        set_scale()
        order_own(1)
        local[6].wait()
        local[7].wait()
        share_all(0, sum(obs_ref[n] * obs_ref[n] for n in range(steps)))

        def sources_of(e, n):
            residual = records(e) - obs_ref[n - 1]
            residual_h = records_h(e) - halo_obs[n - 1]
            whole = spread(residual / mean_square, row_mask, lane_mask)
            inject[n - 1, 0:4] = whole.reshape(4, 4, 4, 8, ez)
            whole = spread(residual_h / mean_square, row_mask_h, lane_mask_h)
            inject[n - 1, 4] = whole.reshape(4, 4, 8, ez)
            return residual * residual

        residual_sum = jnp.zeros((1, ez), F32)
        receive(fu, 0)
        advance(u.at[1], u.at[0], before.at[0], fu)
        fill(u.at[1])
        for n in range(1, last):
            stencil(u.at[n], fu, store=grads.at[n])
            assemble(fu, n)
            if n == 1:
                order_halo(1)
                fill(lam.at[0])
                stencil(lam.at[0], fl, store=grads.at[last])
                assemble(fl, steps)
                order_own(3)
                order_halo(3)
                masks(rec_ref[...], row_mask, lane_mask, False)
                halo_wait([5, 6])
                masks(halo_rec[...], row_mask_h, lane_mask_h, True)
                energy = take_all(0)
                mean_square = energy / samples + EPSILON
            residual_sum = residual_sum + sources_of(u.at[n], n)
            receive(fu, n)
            advance(u.at[n + 1], u.at[n], u.at[n - 1], fu)
        residual_sum = residual_sum + sources_of(u.at[last], last)
        receive(fl, steps)

        for k, n in enumerate(range(last, 0, -1)):
            for p in range(5):
                fl[p, 0:4, 0:4] = fl[p, 0:4, 0:4] - inject[n - 1, p]
            advance(lam.at[k + 1], lam.at[k], before.at[1] if k == 0 else lam.at[k - 1], fl)
            fill(lam.at[k + 1])
            if n - 1 > 0:
                stencil(lam.at[k + 1], fl, partner=grads.at[n - 1], fresh=k == 0)
                assemble(fl, steps + 1 + k)
                if k == 0:
                    fill(u.at[last])
                    stencil(u.at[last], fu, partner=grads.at[last])
                    assemble(fu, last)
                receive(fl, steps + 1 + k)
        stencil(lam.at[last], None, partner=grads.at[0])

        flat_total = total.reshape(125 * 8, ez)
        beside = event + 1 - 2 * lax.rem(event, 2)
        across = lax.rem(event + 2, events)
        beyond = lax.rem(beside + 2, events)
        for owner in range(events):
            for i in range(ex):
                pack[owner, i, 120:128] = jnp.zeros((8, ez), F32)
                pack[owner, i, 0:125] = flat_total[pl.ds(i * ey + owner, 125, stride=8), :]

        def reduce_copy(src, slot, there):
            return pltpu.make_async_remote_copy(
                src_ref=src, dst_ref=got.at[slot], send_sem=red_s.at[slot], recv_sem=red_r.at[slot],
                device_id={"event": there}, device_id_type=MESH,
            )

        first = reduce_copy(pack.at[beyond], 0, beside)
        second = reduce_copy(pack.at[beside], 1, beside)
        first.start()
        second.start()
        first.wait()
        relay[...] = pack[across] + got[0]
        third = reduce_copy(relay, 2, across)
        third.start()

        receive(fu, last)
        u3 = u.at[steps]
        advance(u3, u.at[last], u.at[last - 1] if last > 0 else before.at[0], fu, count=4)
        residual = records(u3) - obs_ref[last]
        share_all(1, residual_sum + residual * residual)

        @pl.when(has_left)
        def _():
            for copy in halo_copies:
                copy.wait_send()


        second.wait()
        pair_sum = pack[event] + got[1]
        third.wait()
        value = (pair_sum + got[2]) * cube_ref[...][None]
        final[...] = value

        top = jnp.max(jnp.abs(value).reshape(ex * 16, 8, ez), axis=0)
        tops_out[0] = top
        tops_in[event] = top
        for k in range(1, events):
            pltpu.make_async_remote_copy(
                src_ref=tops_out.at[0], dst_ref=tops_in.at[event],
                send_sem=top_s.at[k], recv_sem=top_r.at[event],
                device_id={"event": lax.rem(event + k, events)}, device_id_type=MESH,
            ).start()
        for k in range(1, events):
            there = lax.rem(event + k, events)
            copy = pltpu.make_async_remote_copy(
                src_ref=tops_out.at[0], dst_ref=tops_in.at[there],
                send_sem=top_s.at[k], recv_sem=top_r.at[there],
                device_id={"event": there}, device_id_type=MESH,
            )
            copy.wait_send()
            copy.wait_recv()
        top = jnp.max(tops_in[...], axis=0)
        tops_out[1] = top
        tops_far[me] = top

        @pl.loop(1, spaces)
        def _(k):
            pltpu.make_async_remote_copy(
                src_ref=tops_out.at[1], dst_ref=tops_far.at[me],
                send_sem=far_s.at[k], recv_sem=far_r.at[me],
                device_id={"space": lax.rem(me + k, spaces)}, device_id_type=MESH,
            ).start()

        misfit_sum = take_all(1)
        misfit = 0.5 * misfit_sum / (samples * mean_square)
        side_ref[...] = jnp.broadcast_to(misfit, (1, ez))

        @pl.loop(1, spaces)
        def _(k):
            there = lax.rem(me + k, spaces)
            copy = pltpu.make_async_remote_copy(
                src_ref=tops_out.at[1], dst_ref=tops_far.at[there],
                send_sem=far_s.at[k], recv_sem=far_r.at[there],
                device_id={"space": there}, device_id_type=MESH,
            )
            copy.wait_send()
            copy.wait_recv()

        top = jnp.max(tops_far[...], axis=0)
        top = jnp.max(jnp.max(top, axis=1, keepdims=True), axis=0, keepdims=True)
        value = final[...] * (1.0 / (top + EPSILON))[None]
        for p in range(5):
            for i in range(ex):
                at = (p * ex + i) * 25
                out_ref[at : at + 25, 0, :] = value[i, p * 25 : p * 25 + 25, :]

    return kernel


def shards(mesh_shape, now, prev, adj, nxt, modulus, density, receivers, observed):
    events, spaces = mesh_shape["event"], mesh_shape["space"]
    ex, ey, ez = modulus.shape[1], modulus.shape[3], modulus.shape[5]
    steps, count = observed.shape[1], receivers.shape[0]
    assert ex * ey == 8 and ex == 2 and ez == 128 and count == 128 and events == 4 == ey
    assert steps >= 3 and now.shape[0] == 1
    ny, nz = now.shape[2], now.shape[3]
    kernel = make_kernel(ex, ey, ez, steps, events, spaces, count * spaces)
    vm = lambda *shape: pltpu.VMEM(shape, F32)
    dma = lambda *shape: pltpu.SemaphoreType.DMA(shape)
    rounds = 2 * steps
    scratch = [
        vm(5, 4 * ex, ny, nz), vm(5, ex, 5, 5, ey, ez), pltpu.VMEM((1, count), jnp.int32),
        vm(steps, 1, count), pltpu.VMEM((2 * ez, 2 * ez), BF16), vm(4, 4 * ex * ny, ez),
        vm(128, ez), dma(8),
        vm(5, ny, nz), pltpu.VMEM((1, count), jnp.int32), vm(steps, 1, count),
        vm(steps + 1, 5, 5, 5, 8, ez), vm(steps, 5, 5, 5, 8, ez), vm(2, 5, 4, 4, 8, ez),
        vm(5, 4, 4, 8, ez), vm(5, 5, 5, 8, ez), vm(steps, 3, 5, 5, 5, 8, ez),
        vm(2, 5, 5, 5, 8, ez), vm(5, 5, 5, 8, ez), vm(steps - 1, 5, 4, 4, 8, ez),
        vm(512, count), pltpu.VMEM((ez, count), BF16), vm(128, count),
        pltpu.VMEM((ez, count), BF16),
        vm(rounds, 2, 4, 8, ez), vm(rounds, 2, 4, 8, ez),
        vm(rounds, 2, 4, 8, ez), vm(rounds, 2, 4, 8, ez),
        vm(2, 8, ez), vm(2, spaces, 8, ez), vm(events, ex, 128, ez), vm(3, ex, 128, ez),
        vm(ex, 128, ez), vm(2, 8, ez), vm(events, 8, ez), vm(spaces, 8, ez), vm(ex, 128, ez),
        dma(7), dma(7), dma(rounds), dma(rounds), dma(rounds), dma(rounds),
        dma(2, spaces), dma(2, spaces), dma(3), dma(3),
        dma(events), dma(events), dma(spaces), dma(spaces),
    ]
    vmem = pl.BlockSpec(memory_space=pltpu.VMEM)
    hbm = pl.BlockSpec(memory_space=pltpu.HBM)
    out, side = pl.pallas_call(
        kernel,
        out_shape=(
            jax.ShapeDtypeStruct((25 * 5 * ex, 1, ez), F32),
            jax.ShapeDtypeStruct((1, ez), F32),
        ),
        in_specs=[hbm] * 8,
        out_specs=(vmem, vmem),
        scratch_shapes=scratch,
        compiler_params=pltpu.CompilerParams(
            collective_id=0, has_side_effects=True, vmem_limit_bytes=LIMIT
        ),
        name="window",
    )(
        now, prev, adj, nxt, density, jnp.transpose(modulus, (0, 1, 2, 4, 3, 5)),
        receivers.reshape(1, count), jnp.transpose(observed, (1, 0, 2)),
    )
    out = jnp.transpose(out.reshape(5, ex, 5, 5, 1, ez), (0, 1, 2, 4, 3, 5))
    return out, side[0, :1]


def solution(mesh):
    in_specs = (
        P("event", "space", None, None),
        P("event", "space", None, None),
        P("event", "space", None, None),
        P("event", "space", None, None),
        P(None, "space", None, None, None, None),
        P("space", None, None),
        P("space"),
        P("event", None, "space"),
    )
    out_specs = (P(None, "space", None, "event", None, None), P("event"))
    sizes = dict(mesh.shape)

    def program(*args):
        return shards(sizes, *args)

    return jax.shard_map(program, mesh=mesh, in_specs=in_specs, out_specs=out_specs, check_vma=False)
```
